128 devices in a mesh: seq: 8 (over z, core), tp: 16 (over x, y).
Axes of the slice: x: 4, y: 4, z: 4, core: 2. Of those that a mesh axis runs over, the one named last changes fastest.
Arguments:
- new_tokens: bfloat16 [64, 8, 8192], P(None, 'seq'), may hold values from -6 to 6
- norm_gain: float32 [8192], replicated, may hold values from 0.5 to 1.5
- query_weight: bfloat16 [8192, 8192], P(None, 'tp'), may hold values from -1 to 1
- key_weight: bfloat16 [8192, 1024], P(None, 'tp'), may hold values from -1 to 1
- value_weight: bfloat16 [8192, 1024], P(None, 'tp'), may hold values from -0.0625 to 0.0625
- kv_cache: bfloat16 [2, 8, 32768, 1024], P(None, None, ('seq', 'tp')), may hold values from -20 to 20, as said below
- kept_blocks: int32 [8, 8, 256], replicated, may hold values from 0 to 511, as said below
- kept_counts: int32 [8, 8], replicated, may hold values from 2 to 256, as said below
Outputs:
- attended: bfloat16 [64, 8, 8192], P(None, 'seq', 'tp')
- new_entries: bfloat16 [8, 16, 16384], P('seq', 'tp')
The draws below stay inside these ranges and needn't reach their ends.
Inputs may be any that keep to these rules, and one draw needn't show every extreme that they name: `kv_cache`: index 0 of the first dimension holds keys, index 1 values. `kept_blocks`: for each prompt and KV head the first kept_counts entries are distinct block numbers in ascending order and the rest are 0. Among the 4 blocks of a prompt that one device of seq+tp holds, at most 2 are kept for one KV head; in every draw some prompt and head keeps exactly 2 on every device, and every prompt and head keeps exactly 2 on some device. `kept_counts`: the number of valid entries of kept_blocks for each prompt and KV head.
All inputs are finite; a program needn't handle non-finite values.
Results may differ from the reference program's by a relative error of at most 0.012.
Values may be sent and summed in bfloat16 or wider, within the bound.
A program may use at most 128 MiB of HBM per device.

```python
import math
import jax
import jax.numpy as jnp
from jax import lax

D = 8192
H = 64
KVH = 8
HD = 128
BLOCK = 64
CAP = 2
STEPS = 64
TOKD = 256
B = 8
LEN = 32768
NB = 512
MAXK = 256
N_SEQ = 8
N_TP = 16


def kept_layout(key):
    blocks_each = TOKD // BLOCK
    sources = N_SEQ * N_TP
    all_blocks = LEN // BLOCK
    key_heavy, key_pair, key_count, key_source, key_order = jax.random.split(key, 5)
    pair_ids = jnp.arange(B * KVH, dtype=jnp.int32).reshape(B, KVH, 1)
    heavy_pair = jax.random.randint(key_heavy, (B, KVH, 1), 0, 4) == 0
    heavy_pair = heavy_pair | (pair_ids == jax.random.randint(key_pair, (), 0, B * KVH))
    counts_each = jax.random.randint(key_count, (B, KVH, sources), 0, CAP + 1)
    forced = jax.random.randint(key_source, (B, KVH, 1), 0, sources)
    source_ids = jnp.arange(sources, dtype=jnp.int32)[None, None, :]
    counts_each = jnp.where(heavy_pair | (source_ids == forced), CAP, counts_each)
    base_order = jnp.broadcast_to(jnp.arange(blocks_each, dtype=jnp.int32), (B, KVH, sources, blocks_each))
    block_order = jax.random.permutation(key_order, base_order, axis=3, independent=True)
    chosen = (block_order < counts_each[..., None]).reshape(B, KVH, all_blocks)
    slot_place = jnp.cumsum(chosen.astype(jnp.int32), axis=2) - 1
    slot_place = jnp.where(chosen, slot_place, CAP * sources)
    prompt_ids = jnp.broadcast_to(jnp.arange(B, dtype=jnp.int32)[:, None, None], (B, KVH, all_blocks))
    head_ids = jnp.broadcast_to(jnp.arange(KVH, dtype=jnp.int32)[None, :, None], (B, KVH, all_blocks))
    block_ids = jnp.broadcast_to(jnp.arange(all_blocks, dtype=jnp.int32)[None, None, :], (B, KVH, all_blocks))
    kept_lists = jnp.zeros((B, KVH, CAP * sources), jnp.int32)
    kept_lists = kept_lists.at[prompt_ids, head_ids, slot_place].set(block_ids, mode='drop')
    kept_totals = jnp.sum(chosen.astype(jnp.int32), axis=2)
    return (kept_lists, kept_totals)


def draw_kept_blocks(key, part):
    kept_lists, kept_totals = kept_layout(key)
    return kept_lists


def draw_kept_counts(key, part):
    kept_lists, kept_totals = kept_layout(key)
    return kept_totals


def draw_new_tokens(key, part):
    key = jax.random.fold_in(key, 23)
    shape = (STEPS, B, D)
    values = jnp.clip(jax.random.normal(key, shape, jnp.float32), -6.0, 6.0)
    return values.astype(jnp.bfloat16)


def draw_query_weight(key, part):
    key = jax.random.fold_in(key, 37)
    shape = (D, H * HD)
    values = jnp.clip(jax.random.normal(key, shape, jnp.float32), -5.0, 5.0) / math.sqrt(D)
    return values.astype(jnp.bfloat16)


def draw_key_weight(key, part):
    key = jax.random.fold_in(key, 53)
    shape = (D, KVH * HD)
    values = jnp.clip(jax.random.normal(key, shape, jnp.float32), -5.0, 5.0) / math.sqrt(D)
    return values.astype(jnp.bfloat16)


def draw_kv_cache(key, part):
    key = jax.random.fold_in(key, 11)
    key_base = jax.random.fold_in(key, 0)
    shape = (2, B, LEN, KVH * HD)
    kind_scale = jnp.array([2.5, 4.0], jnp.float32)[:, None, None, None]
    base = jnp.clip(jax.random.normal(key_base, shape, jnp.float32), -5.0, 5.0)
    values = base * kind_scale
    return values.astype(jnp.bfloat16)


def block_scale(own_key, extent, cuts, smallest, largest):
    level = 1.0
    for axis_at, blocks in cuts:
        steps = jax.random.uniform(jax.random.fold_in(jax.random.fold_in(own_key, 6), axis_at), (blocks,), jnp.float32, smallest / len(cuts), largest / len(cuts))
        level = level * jnp.repeat(jnp.exp(steps), extent[axis_at] // blocks).reshape((-1,) + (1,) * (len(extent) - 1 - axis_at))
    return level


def bell_draw(own_key, extent, spread, reach, pieces=(), held_as=jnp.bfloat16):
    result = jax.random.normal(own_key, extent, jnp.float32) * spread
    if len(pieces) > 0:
        result = block_scale(own_key, extent, pieces, -0.22, 0.18) * result
    return jnp.clip(result, min=-reach, max=reach).astype(held_as)


def setup_inputs(seed: int = 0) -> dict:
    keys = jax.random.split(jax.random.key(seed), 9)
    return {
        "new_tokens": draw_new_tokens(jax.random.fold_in(keys[8], 71), 0),
        "norm_gain": jnp.clip(1.0 + 0.1 * jax.random.normal(keys[1], (D,), jnp.float32), 0.5, 1.5),
        "query_weight": draw_query_weight(jax.random.fold_in(keys[8], 71), 0),
        "key_weight": draw_key_weight(jax.random.fold_in(keys[8], 71), 0),
        "value_weight": bell_draw(keys[4], (D, KVH * HD), D ** -0.5, 0.0625, ((1, 16),)),
        "kv_cache": draw_kv_cache(jax.random.fold_in(keys[8], 71), 0),
        "kept_blocks": draw_kept_blocks(jax.random.fold_in(keys[8], 71), 0),
        "kept_counts": draw_kept_counts(jax.random.fold_in(keys[8], 71), 0),
    }


def scaled_norm(tokens, norm_gain):
    values = tokens.astype(jnp.float32)
    mean_square = lax.optimization_barrier(jnp.mean(values * values, axis=-1, keepdims=True))
    return (values * lax.rsqrt(mean_square + 1e-05) * norm_gain).astype(jnp.bfloat16)

def reference(new_tokens, norm_gain, query_weight, key_weight, value_weight, kv_cache, kept_blocks, kept_counts):
    group_size = H // KVH
    copies = N_TP // KVH
    score_scale = 1.0 / math.sqrt(HD)
    normed = scaled_norm(new_tokens, norm_gain).reshape(STEPS * B, D)
    queries = jnp.dot(normed, query_weight, preferred_element_type=jnp.float32).astype(jnp.bfloat16)
    queries = queries.reshape(STEPS, B, H, HD)
    new_keys = jnp.dot(normed, key_weight, preferred_element_type=jnp.float32).astype(jnp.bfloat16)
    new_keys = new_keys.reshape(STEPS, B, KVH, HD)
    new_values = jnp.dot(normed, value_weight, preferred_element_type=jnp.float32).astype(jnp.bfloat16)
    new_values = new_values.reshape(STEPS, B, KVH, HD)
    per_head = jnp.stack([new_keys, new_values]).transpose(2, 3, 0, 1, 4).reshape(B, KVH, 2 * STEPS * HD)
    new_entries = jnp.repeat(per_head, copies, axis=1)
    causal = jnp.arange(STEPS, dtype=jnp.int32)[None, :] <= jnp.arange(STEPS, dtype=jnp.int32)[:, None]
    slot_ids = jnp.arange(MAXK, dtype=jnp.int32)

    def one_pair(pair_index):
        prompt_id = pair_index // KVH
        head_id = pair_index % KVH
        block_list = kept_blocks[prompt_id, head_id]
        live_mask = slot_ids < kept_counts[prompt_id, head_id]
        prompt_cache = lax.dynamic_index_in_dim(kv_cache, prompt_id, 1, keepdims=False)
        head_cache = lax.dynamic_slice_in_dim(prompt_cache, head_id * HD, HD, 2).reshape(2, NB, BLOCK, HD)
        kept_rows = jnp.take(head_cache, block_list, axis=1).astype(jnp.float32)
        prompt_queries = lax.dynamic_index_in_dim(queries, prompt_id, 1, keepdims=False)
        head_queries = lax.dynamic_slice_in_dim(prompt_queries, head_id * group_size, group_size, 1).astype(jnp.float32)
        prompt_keys = lax.dynamic_index_in_dim(new_keys, prompt_id, 1, keepdims=False)
        own_keys = lax.dynamic_index_in_dim(prompt_keys, head_id, 1, keepdims=False).astype(jnp.float32)
        prompt_values = lax.dynamic_index_in_dim(new_values, prompt_id, 1, keepdims=False)
        own_values = lax.dynamic_index_in_dim(prompt_values, head_id, 1, keepdims=False).astype(jnp.float32)
        cache_scores = jnp.einsum('sgd,mtd->sgmt', head_queries, kept_rows[0]) * score_scale
        cache_scores = jnp.where(live_mask[None, None, :, None], cache_scores, -1e+30)
        own_scores = jnp.einsum('sgd,ud->sgu', head_queries, own_keys) * score_scale
        own_scores = jnp.where(causal[:, None, :], own_scores, -1e+30)
        row_top = jnp.maximum(lax.optimization_barrier(jnp.max(cache_scores, axis=(2, 3))), lax.optimization_barrier(jnp.max(own_scores, axis=2)))
        cache_exp = jnp.exp(cache_scores - row_top[:, :, None, None])
        own_exp = jnp.exp(own_scores - row_top[:, :, None])
        row_total = lax.optimization_barrier(jnp.sum(cache_exp, axis=(2, 3))) + lax.optimization_barrier(jnp.sum(own_exp, axis=2))
        cache_weights = (cache_exp / row_total[:, :, None, None]).astype(jnp.bfloat16).astype(jnp.float32)
        own_weights = (own_exp / row_total[:, :, None]).astype(jnp.bfloat16).astype(jnp.float32)
        head_output = jnp.einsum('sgmt,mtd->sgd', cache_weights, kept_rows[1])
        head_output = head_output + jnp.einsum('sgu,ud->sgd', own_weights, own_values)
        return head_output.astype(jnp.bfloat16)
    outputs = lax.map(one_pair, jnp.arange(B * KVH, dtype=jnp.int32))
    attended = outputs.reshape(B, KVH, STEPS, group_size, HD).transpose(2, 0, 1, 3, 4).reshape(STEPS, B, H * HD)
    return (attended, new_entries)
```

```python
import math

import jax
import jax.numpy as jnp
from jax import lax
from jax.experimental import pallas as pl
from jax.experimental.pallas import tpu as pltpu
from jax.sharding import PartitionSpec as P

HD = 128
BLOCK = 64
CAP = 2
STEPS = 64
KEYS = CAP * BLOCK
TOKD = 256
WIDTH = 8192
SLOTS = 4
SOURCES = 16
SITES = 8
GROUP = 256
CHUNKS = 8
CHUNK = WIDTH // CHUNKS
MESH = pl.DeviceIdType.MESH
EXP_SCALE = math.log2(math.e) / math.sqrt(HD)
LOWEST = -1e30

NT = (((1,), (1,)), ((), ()))
TN = (((0,), (0,)), ((), ()))


def kernel(
    tok_hbm,
    gain_ref,
    wq_hbm,
    wk_hbm,
    wv_hbm,
    kv_hbm,
    kept_ref,
    counts_ref,
    att_ref,
    ent_ref,
    kv_buf,
    packed,
    recv,
    tok,
    normed,
    wq,
    wkv,
    q_acc,
    n_acc,
    q_send,
    q_buf,
    pick,
    live_keys,
    s_buf,
    p_buf,
    o_send,
    l_send,
    o_buf,
    l_buf,
    own_o,
    own_l,
    piece,
    other,
    kv_sem,
    w_sem,
    tok_sem,
    pack_sem,
    recv_sem,
    q_send_sem,
    q_recv_sem,
    o_send_sem,
    o_recv_sem,
    l_send_sem,
    l_recv_sem,
    piece_sem,
):
    seq = lax.axis_index("seq")
    tp = lax.axis_index("tp")
    z, c = seq // 2, seq % 2
    x, y = tp // 4, tp % 4
    flat = seq * 16 + tp

    def device(x_, y_, z_, c_):
        return (z_ * 2 + c_, x_ * 4 + y_)

    kv_copies = []
    for t in range(SLOTS):
        u, v = t // 2, t % 2
        kv_copies.append(
            pltpu.make_async_copy(
                kv_hbm.at[:, pl.ds(4 * u, 4), :, pl.ds(512 * v, 512)], kv_buf.at[t], kv_sem.at[t]
            )
        )
        kv_copies[t].start()
    tok_copy = pltpu.make_async_copy(tok_hbm, tok, tok_sem)
    wk_copy = pltpu.make_async_copy(wk_hbm, wkv.at[pl.ds(0, 64)], w_sem.at[CHUNKS])
    wv_copy = pltpu.make_async_copy(wv_hbm, wkv.at[pl.ds(64, 64)], w_sem.at[CHUNKS + 1])

    def wq_copy(k):
        rows = pl.ds(pl.multiple_of(k * CHUNK, CHUNK), CHUNK)
        return pltpu.make_async_copy(wq_hbm.at[rows], wq.at[rows], w_sem.at[k])

    barrier = pltpu.get_barrier_semaphore()

    def greet_near(i, carry):
        c_ = (c + i) % 2
        z_ = (z + (i // 2) % 3 + 3) % 4
        y_ = (y + (i // 6) % 3 + 3) % 4
        x_ = (x + i // 18 + 3) % 4

        @pl.when(i != 26)
        def _():
            pl.semaphore_signal(
                barrier, inc=1, device_id=device(x_, y_, z_, c_), device_id_type=MESH
            )

        return carry

    lax.fori_loop(0, 54, greet_near, 0)

    def greet_far(i, carry):
        y_ = (y + i % 4) % 4
        z_ = (z + 2 * ((i // 4) % 2)) % 4
        x_ = (x + 2 * (i // 8)) % 4
        pl.semaphore_signal(barrier, inc=1, device_id=device(x_, y_, z_, c), device_id_type=MESH)
        return carry

    lax.fori_loop(1, 16, greet_far, 0)

    lane = lax.broadcasted_iota(jnp.int32, (8, 256), 1)
    eye = lax.broadcasted_iota(jnp.int32, (8, 8), 0) == lax.broadcasted_iota(jnp.int32, (8, 8), 1)
    lane_8 = lax.broadcasted_iota(jnp.int32, (1, 8), 1)
    for p in range(8):
        count = jnp.sum(jnp.where(eye, counts_ref[pl.ds(p, 1), :], 0), axis=1, keepdims=True)
        rel = kept_ref[p] - 4 * flat
        code = jnp.where(rel == 0, 1, jnp.where(rel == 1, 2, jnp.where(rel == 2, 4, 8)))
        code = jnp.where((rel >= 0) & (rel < 4) & (lane < count), code, 0)
        mask = jnp.sum(code, axis=1, keepdims=True)
        h0, h1, h2 = mask & 1, (mask >> 1) & 1, (mask >> 2) & 1
        first = jnp.where(h0 == 1, 0, jnp.where(h1 == 1, 1, jnp.where(h2 == 1, 2, 3)))
        second = jnp.where(h0 + h1 == 2, 1, jnp.where((h0 + h1 == 1) & (h2 == 1), 2, 3))
        pick[0, pl.ds(8 * p, 8), :] = jnp.broadcast_to(first, (8, HD))
        pick[1, pl.ds(8 * p, 8), :] = jnp.broadcast_to(second, (8, HD))
    source = lax.broadcasted_iota(jnp.int32, (SOURCES, 256), 0)
    lane_16 = lax.broadcasted_iota(jnp.int32, (SOURCES, 256), 1)
    sx, sy = source >> 3, (source >> 2) & 1
    sz, sc = (source >> 1) & 1, source & 1
    for t in range(SLOTS):
        u, v = t // 2, t % 2
        ax, ay, az = (u + y) % 2, (v + z) % 2, (u + v + x) % 2
        nx = (x + 5 - 2 * ((x + ax) % 2)) % 4
        ny = (y + 5 - 2 * ((y + ay) % 2)) % 4
        nz = (z + 5 - 2 * ((z + az) % 2)) % 4
        fx = jnp.where(sx == 0, x, nx)
        fy = jnp.where(sy == 0, y, ny)
        fz = jnp.where(sz == 0, z, nz)
        fc = jnp.where(sc == 0, c, 1 - c)
        owner = (fz * 2 + fc) * 16 + fx * 4 + fy
        p_ = 2 * (2 * u + z % 2) + c
        h_ = 2 * (2 * v + x % 2) + (y + u + v) % 2
        row = kept_ref[p_, pl.ds(h_, 1), :]
        counts = jnp.where(lane_8 == h_, counts_ref[pl.ds(p_, 1), :], 0)
        live = lane_16 < jnp.sum(counts, axis=1, keepdims=True)
        here = jnp.where(live & ((row >> 2) == owner), 1, 0)
        live_keys[pl.ds(16 * t, 16), :] = jnp.broadcast_to(
            BLOCK * jnp.sum(here, axis=1, keepdims=True), (SOURCES, 2 * GROUP)
        )
    pl.semaphore_wait(barrier, 68)

    def pack(t, cls, dst):
        u, v = t // 2, t % 2
        rx = (x + cls // 8) % 2
        ry = (y + cls // 4) % 2
        rz = (z + cls // 2) % 2
        rc = (c + cls) % 2
        p_loc = 2 * rz + rc
        h_loc = 2 * rx + (ry + u + v) % 2
        pair = (4 * u + p_loc) * 8 + 4 * v + h_loc
        columns = pl.ds(pl.multiple_of(h_loc * HD, HD), HD)
        for slot in range(CAP):
            chosen = jnp.broadcast_to(pick[slot, pl.ds(pair, 1), :], (16, HD))
            part = [None, None]
            for block in range(slot, 4):
                weight = jnp.where(chosen == block, 1.0, 0.0).astype(jnp.bfloat16)
                weight = jnp.concatenate([weight] * (BLOCK // 16), axis=0)
                for kind in range(2):
                    rows = kv_buf[t, kind, p_loc, pl.ds(block * BLOCK, BLOCK), columns] * weight
                    part[kind] = rows if part[kind] is None else part[kind] + rows
            for kind in range(2):
                dst[kind, pl.ds(slot * BLOCK, BLOCK), :] = part[kind]

    for t in range(SLOTS):
        u, v = t // 2, t % 2
        kv_copies[t].wait()

        def send(cls, carry, t=t, u=u, v=v):
            dx, dy, dz, dc = cls // 8, (cls // 4) % 2, (cls // 2) % 2, cls % 2
            rx, ry, rz, rc = (x + dx) % 2, (y + dy) % 2, (z + dz) % 2, (c + dc) % 2
            ax, ay, az = (u + ry) % 2, (v + rz) % 2, (u + v + rx) % 2
            x_ = (x + dx * (1 - 2 * ((x + ax) % 2)) + 4) % 4
            y_ = (y + dy * (1 - 2 * ((y + ay) % 2)) + 4) % 4
            z_ = (z + dz * (1 - 2 * ((z + az) % 2)) + 4) % 4
            place = t * 15 + cls - 1
            pack(t, cls, packed.at[place])
            pltpu.make_async_remote_copy(
                src_ref=packed.at[place],
                dst_ref=recv.at[t, cls],
                send_sem=pack_sem,
                recv_sem=recv_sem.at[t],
                device_id=device(x_, y_, z_, rc),
                device_id_type=MESH,
            ).start()
            return carry

        lax.fori_loop(1, SOURCES, send, 0)
        if t == 0:
            tok_copy.start()
            wk_copy.start()
            wv_copy.start()
            for k in range(CHUNKS):
                wq_copy(k).start()
    for t in range(SLOTS):
        pack(t, 0, recv.at[t, 0])

    tok_copy.wait()

    def norm(i, carry):
        rows = pl.ds(pl.multiple_of(i * 16, 16), 16)
        values = tok[rows, :].astype(jnp.float32)
        mean_square = jnp.mean(values * values, axis=-1, keepdims=True)
        normed[rows, :] = (values * lax.rsqrt(mean_square + 1e-05) * gain_ref[...]).astype(
            jnp.bfloat16
        )
        return carry

    lax.fori_loop(0, STEPS // 16, norm, 0)
    wk_copy.wait()
    wv_copy.wait()
    n_acc[...] = jnp.zeros_like(n_acc)
    q_acc[...] = jnp.zeros_like(q_acc)

    def project(k, carry):
        columns = pl.ds(pl.multiple_of(k * CHUNK, CHUNK), CHUNK)
        wq_copy(k).wait()
        rows = normed[:, columns]
        q_acc[...] += jnp.dot(rows, wq[columns, :], preferred_element_type=jnp.float32)
        n_acc[...] += lax.dot_general(rows, wkv[:, columns], NT, preferred_element_type=jnp.float32)
        return carry

    lax.fori_loop(0, CHUNKS, project, 0)

    mine = n_acc[...].astype(jnp.bfloat16)
    piece[...] = mine
    piece_copy = pltpu.make_async_remote_copy(
        src_ref=piece,
        dst_ref=other,
        send_sem=piece_sem.at[0],
        recv_sem=piece_sem.at[1],
        device_id=device(x, y + 1 - 2 * (y % 2), z, c),
        device_id_type=MESH,
    )
    piece_copy.start()
    for g in range(4):
        q_send[pl.ds(g * STEPS, STEPS), :] = q_acc[:, g * HD : (g + 1) * HD].astype(jnp.bfloat16)
    half = y % 2
    home_slot = 2 * (z // 2) + x // 2
    home_parity = (y // 2 + z // 2 + x // 2) % 2
    stays = half == home_parity

    def q_copy(i):
        bx, by, bz = i // 4, (i // 2) % 2, i % 2
        return pltpu.make_async_remote_copy(
            src_ref=q_send,
            dst_ref=q_buf.at[home_slot, half],
            send_sem=q_send_sem.at[i],
            recv_sem=q_recv_sem.at[home_slot, half],
            device_id=device((x + 2 * bx) % 4, home_parity + 2 * by, (z + 2 * bz) % 4, c),
            device_id_type=MESH,
        )

    def is_self(i):
        return (i // 4 == 0) & (i % 2 == 0) & (home_parity + 2 * ((i // 2) % 2) == y)

    def q_start(i, carry):
        @pl.when(jnp.logical_not(is_self(i)))
        def _():
            q_copy(i).start()

        @pl.when(is_self(i))
        def _():
            q_buf[home_slot, half] = q_send[...]

        return carry

    lax.fori_loop(0, SITES, q_start, 0)

    piece_copy.wait()
    mine = piece[...].astype(jnp.float32)
    theirs = other[...].astype(jnp.float32)
    low = jnp.where(half == 0, mine, theirs)
    high = jnp.where(half == 0, theirs, mine)
    first_half = lax.broadcasted_iota(jnp.int32, (STEPS, HD), 1) < 64
    new_keys = jnp.where(first_half, low, pltpu.roll(high, 64, 1)).astype(jnp.bfloat16)
    new_values = jnp.where(first_half, pltpu.roll(low, 64, 1), high).astype(jnp.bfloat16)
    ent_ref[pl.ds(0, STEPS), :] = new_keys
    ent_ref[pl.ds(STEPS, STEPS), :] = new_values
    scores = lax.dot_general(new_keys, q_send[...], NT, preferred_element_type=jnp.float32)
    key_step = lax.broadcasted_iota(jnp.int32, (STEPS, GROUP), 0)
    row_step = lax.broadcasted_iota(jnp.int32, (STEPS, GROUP), 1) % STEPS
    scores = jnp.where(key_step <= row_step, scores, LOWEST)
    top = jnp.max(scores, axis=0, keepdims=True)
    weights = jnp.exp2((scores - top) * EXP_SCALE)
    own_l[...] = jnp.broadcast_to(
        top * EXP_SCALE + jnp.log2(jnp.sum(weights, axis=0, keepdims=True)), (8, GROUP)
    )
    own_o[...] = lax.dot_general(
        new_values, weights.astype(jnp.bfloat16), TN, preferred_element_type=jnp.float32
    ) / jnp.sum(weights, axis=0, keepdims=True)

    key_row = lax.broadcasted_iota(jnp.int32, (KEYS, 2 * GROUP), 0)

    def home_of(t):
        u, v = t // 2, t % 2
        x0, z0 = 2 * v + x % 2, 2 * u + z % 2
        hlo = (y + u + v) % 2
        near = (x0 == x) & (z0 == z) & (hlo == y // 2)
        bx, bz = (x + 4 - x0) // 2 % 2, (z + 4 - z0) // 2 % 2
        return x0, z0, hlo, near, bx * 4 + (y // 2) * 2 + bz

    def out_copies(t, m):
        x0, z0, hlo, _, site = home_of(t)
        home = device(x0, 2 * hlo + m, z0, c)
        return (
            pltpu.make_async_remote_copy(
                src_ref=o_send.at[t, m],
                dst_ref=o_buf.at[site],
                send_sem=o_send_sem.at[t, m],
                recv_sem=o_recv_sem.at[site],
                device_id=home,
                device_id_type=MESH,
            ),
            pltpu.make_async_remote_copy(
                src_ref=l_send.at[t, m],
                dst_ref=l_buf.at[site],
                send_sem=l_send_sem.at[t, m],
                recv_sem=l_recv_sem.at[site],
                device_id=home,
                device_id_type=MESH,
            ),
        )

    def attend(t, carry):
        x0, z0, hlo, near, site = home_of(t)
        for m in range(2):

            @pl.when(jnp.logical_not(near & (y % 2 == m)))
            def _(m=m):
                pltpu.make_async_copy(
                    q_buf.at[t, m], q_buf.at[t, m], q_recv_sem.at[t, m]
                ).wait()

        arrived = recv.at[t, pl.ds(1, SOURCES - 1)]
        pltpu.make_async_copy(arrived, arrived, recv_sem.at[t]).wait()
        q = q_buf[t].reshape(2 * GROUP, HD)

        def score(i, top):
            s = lax.dot_general(recv[t, i, 0], q, NT, preferred_element_type=jnp.float32)
            s = jnp.where(key_row < live_keys[pl.ds(16 * t + i, 1), :], s, LOWEST)
            s_buf[pl.ds(pl.multiple_of(i * KEYS, KEYS), KEYS), :] = s
            return jnp.maximum(top, jnp.max(s.reshape(KEYS // 8, 8, 2 * GROUP), axis=0))

        top = lax.fori_loop(
            0, SOURCES, score, jnp.full((8, 2 * GROUP), LOWEST, jnp.float32)
        )
        top = jnp.max(top, axis=0, keepdims=True)

        def weigh(i, total):
            rows = pl.ds(pl.multiple_of(i * KEYS, KEYS), KEYS)
            w = jnp.exp2((s_buf[rows, :] - top) * EXP_SCALE)
            p_buf[rows, :] = w.astype(jnp.bfloat16)
            return total + jnp.sum(w.reshape(KEYS // 8, 8, 2 * GROUP), axis=0)

        total = lax.fori_loop(0, SOURCES, weigh, jnp.zeros((8, 2 * GROUP), jnp.float32))
        total = jnp.sum(total, axis=0, keepdims=True)
        values = recv[t, :, 1].reshape(SOURCES * KEYS, HD)
        o = lax.dot_general(values, p_buf[...], TN, preferred_element_type=jnp.float32)
        o = (o / total).astype(jnp.bfloat16)
        lse = jnp.broadcast_to(top * EXP_SCALE + jnp.log2(total), (8, 2 * GROUP))
        for m in range(2):
            o_send[t, m] = o[:, m * GROUP : (m + 1) * GROUP]
            l_send[t, m] = lse[:, m * GROUP : (m + 1) * GROUP]
            leaves = jnp.logical_not(near & (y % 2 == m))

            @pl.when(leaves)
            def _(m=m):
                for copy in out_copies(t, m):
                    copy.start()

            @pl.when(jnp.logical_not(leaves))
            def _(m=m):
                o_buf[site] = o_send[t, m]
                l_buf[site] = l_send[t, m]

        return carry

    lax.fori_loop(0, SLOTS, attend, 0)

    def await_site(i, carry):
        @pl.when(jnp.logical_not(is_self(i)))
        def _():
            pltpu.make_async_copy(o_buf.at[i], o_buf.at[i], o_recv_sem.at[i]).wait()
            pltpu.make_async_copy(l_buf.at[i], l_buf.at[i], l_recv_sem.at[i]).wait()

        return carry

    lax.fori_loop(0, SITES, await_site, 0)
    top = own_l[pl.ds(0, 1), :]
    for i in range(SITES):
        top = jnp.maximum(top, l_buf[i, pl.ds(0, 1), :])
    share = jnp.exp2(own_l[pl.ds(0, 1), :] - top)
    total = share
    result = own_o[...] * share
    for i in range(SITES):
        share = jnp.exp2(l_buf[i, pl.ds(0, 1), :] - top)
        total = total + share
        result = result + o_buf[i].astype(jnp.float32) * share
    result = (result / total).T
    for g in range(4):
        att_ref[:, g * HD : (g + 1) * HD] = result[g * STEPS : (g + 1) * STEPS, :].astype(
            jnp.bfloat16
        )

    pltpu.make_async_copy(packed, packed, pack_sem).wait()

    def await_q(i, carry):
        @pl.when(jnp.logical_not(is_self(i)))
        def _():
            q_copy(i).wait_send()

        return carry

    lax.fori_loop(0, SITES, await_q, 0)

    def await_out(t, carry):
        _, _, _, near, _ = home_of(t)
        for m in range(2):

            @pl.when(jnp.logical_not(near & (y % 2 == m)))
            def _(m=m):
                for copy in out_copies(t, m):
                    copy.wait_send()

        return carry

    lax.fori_loop(0, SLOTS, await_out, 0)


def per_device(
    new_tokens,
    norm_gain,
    query_weight,
    key_weight,
    value_weight,
    kv_cache,
    kept_blocks,
    kept_counts,
):
    vmem = pl.BlockSpec(memory_space=pltpu.VMEM)
    hbm = pl.BlockSpec(memory_space=pl.ANY)
    bf16, f32 = jnp.bfloat16, jnp.float32
    dma = pltpu.SemaphoreType.DMA
    attended, entries = pl.pallas_call(
        kernel,
        out_shape=(
            jax.ShapeDtypeStruct((STEPS, 4 * HD), bf16),
            jax.ShapeDtypeStruct((2 * STEPS, HD), bf16),
        ),
        in_specs=[hbm, vmem, hbm, hbm, hbm, hbm, vmem, vmem],
        out_specs=(vmem, vmem),
        scratch_shapes=[
            pltpu.VMEM((SLOTS, 2, 4, TOKD, 4 * HD), bf16),
            pltpu.VMEM((SLOTS * (SOURCES - 1), 2, KEYS, HD), bf16),
            pltpu.VMEM((SLOTS, SOURCES, 2, KEYS, HD), bf16),
            pltpu.VMEM((STEPS, WIDTH), bf16),
            pltpu.VMEM((STEPS, WIDTH), bf16),
            pltpu.VMEM((WIDTH, 4 * HD), bf16),
            pltpu.VMEM((HD, WIDTH), bf16),
            pltpu.VMEM((STEPS, 4 * HD), f32),
            pltpu.VMEM((STEPS, HD), f32),
            pltpu.VMEM((GROUP, HD), bf16),
            pltpu.VMEM((SLOTS, 2, GROUP, HD), bf16),
            pltpu.VMEM((CAP, 64, HD), jnp.int32),
            pltpu.VMEM((SLOTS * SOURCES, 2 * GROUP), jnp.int32),
            pltpu.VMEM((SOURCES * KEYS, 2 * GROUP), f32),
            pltpu.VMEM((SOURCES * KEYS, 2 * GROUP), bf16),
            pltpu.VMEM((SLOTS, 2, HD, GROUP), bf16),
            pltpu.VMEM((SLOTS, 2, 8, GROUP), f32),
            pltpu.VMEM((SITES, HD, GROUP), bf16),
            pltpu.VMEM((SITES, 8, GROUP), f32),
            pltpu.VMEM((HD, GROUP), f32),
            pltpu.VMEM((8, GROUP), f32),
            pltpu.VMEM((STEPS, HD), bf16),
            pltpu.VMEM((STEPS, HD), bf16),
            dma((SLOTS,)),
            dma((CHUNKS + 2,)),
            dma,
            dma,
            dma((SLOTS,)),
            dma((SITES,)),
            dma((SLOTS, 2)),
            dma((SLOTS, 2)),
            dma((SITES,)),
            dma((SLOTS, 2)),
            dma((SITES,)),
            dma((2,)),
        ],
        compiler_params=pltpu.CompilerParams(
            collective_id=0, has_side_effects=True, vmem_limit_bytes=56 * 1024 * 1024
        ),
    )(
        new_tokens.reshape(STEPS, WIDTH),
        norm_gain.reshape(1, WIDTH),
        query_weight,
        key_weight.T,
        value_weight.T,
        kv_cache,
        kept_blocks,
        kept_counts,
    )
    return (
        attended.reshape(STEPS, 1, 4 * HD),
        entries.reshape(1, 1, 2 * STEPS * HD),
    )


def solution(mesh):
    in_specs = (
        P(None, "seq", None),
        P(),
        P(None, "tp"),
        P(None, "tp"),
        P(None, "tp"),
        P(None, None, ("seq", "tp"), None),
        P(),
        P(),
    )
    out_specs = (P(None, "seq", "tp"), P("seq", "tp", None))
    return jax.shard_map(
        per_device, mesh=mesh, in_specs=in_specs, out_specs=out_specs, check_vma=False
    )
```

```python
import math

import jax
import jax.numpy as jnp
from jax import lax
from jax.experimental import pallas as pl
from jax.experimental.pallas import tpu as pltpu
from jax.sharding import PartitionSpec as P

HD = 128
BLOCK = 64
CAP = 2
STEPS = 64
KEYS = CAP * BLOCK
TOKD = 256
WIDTH = 8192
SLOTS = 4
SOURCES = 16
SITES = 8
GROUP = 256
CHUNKS = 8
CHUNK = WIDTH // CHUNKS
MESH = pl.DeviceIdType.MESH
EXP_SCALE = math.log2(math.e) / math.sqrt(HD)
LOWEST = -1e30

NT = (((1,), (1,)), ((), ()))
TN = (((0,), (0,)), ((), ()))


def kernel(
    tok_hbm,
    gain_ref,
    wq_hbm,
    wk_hbm,
    wv_hbm,
    kv_hbm,
    kept_ref,
    counts_ref,
    att_ref,
    ent_ref,
    kv_buf,
    packed,
    recv,
    tok,
    normed,
    wq,
    wkv,
    q_acc,
    n_acc,
    q_send,
    q_buf,
    pick,
    live_keys,
    o_send,
    l_send,
    o_buf,
    l_buf,
    own_o,
    own_l,
    piece,
    other,
    kv_sem,
    w_sem,
    tok_sem,
    pack_sem,
    recv_sem,
    q_send_sem,
    q_recv_sem,
    o_send_sem,
    o_recv_sem,
    l_send_sem,
    l_recv_sem,
    piece_sem,
):
    seq = lax.axis_index("seq")
    tp = lax.axis_index("tp")
    z, c = seq // 2, seq % 2
    x, y = tp // 4, tp % 4
    flat = seq * 16 + tp

    def device(x_, y_, z_, c_):
        return (z_ * 2 + c_, x_ * 4 + y_)

    def kv_copy(t):
        u, v = t // 2, t % 2
        return pltpu.make_async_copy(
            kv_hbm.at[:, pl.ds(4 * u, 4), :, pl.ds(512 * v, 512)], kv_buf.at[t], kv_sem.at[t]
        )

    def wq_copy(k):
        rows = pl.ds(pl.multiple_of(k * CHUNK, CHUNK), CHUNK)
        return pltpu.make_async_copy(wq_hbm.at[rows], wq.at[rows], w_sem.at[k])

    tok_copy = pltpu.make_async_copy(tok_hbm, tok, tok_sem)
    wk_copy = pltpu.make_async_copy(wk_hbm, wkv.at[pl.ds(0, 64)], w_sem.at[CHUNKS])
    wv_copy = pltpu.make_async_copy(wv_hbm, wkv.at[pl.ds(64, 64)], w_sem.at[CHUNKS + 1])
    kv_copy(0).start()
    kv_copy(1).start()
    tok_copy.start()
    wk_copy.start()
    wv_copy.start()
    for k in range(CHUNKS):
        wq_copy(k).start()
    kv_copy(2).start()
    kv_copy(3).start()

    barrier = pltpu.get_barrier_semaphore()

    def greet_near(i, carry):
        c_ = (c + i) % 2
        z_ = (z + (i // 2) % 3 + 3) % 4
        y_ = (y + (i // 6) % 3 + 3) % 4
        x_ = (x + i // 18 + 3) % 4

        @pl.when(i != 26)
        def _():
            pl.semaphore_signal(
                barrier, inc=1, device_id=device(x_, y_, z_, c_), device_id_type=MESH
            )

        return carry

    lax.fori_loop(0, 54, greet_near, 0)

    def greet_far(i, carry):
        y_ = (y + i % 4) % 4
        z_ = (z + 2 * ((i // 4) % 2)) % 4
        x_ = (x + 2 * (i // 8)) % 4
        pl.semaphore_signal(barrier, inc=1, device_id=device(x_, y_, z_, c), device_id_type=MESH)
        return carry

    lax.fori_loop(1, 16, greet_far, 0)

    lane = lax.broadcasted_iota(jnp.int32, (8, 256), 1)
    eye = lax.broadcasted_iota(jnp.int32, (8, 8), 0) == lax.broadcasted_iota(jnp.int32, (8, 8), 1)
    lane_8 = lax.broadcasted_iota(jnp.int32, (1, 8), 1)
    for p in range(8):
        count = jnp.sum(jnp.where(eye, counts_ref[pl.ds(p, 1), :], 0), axis=1, keepdims=True)
        rel = kept_ref[p] - 4 * flat
        code = jnp.where(rel == 0, 1, jnp.where(rel == 1, 2, jnp.where(rel == 2, 4, 8)))
        code = jnp.where((rel >= 0) & (rel < 4) & (lane < count), code, 0)
        mask = jnp.sum(code, axis=1, keepdims=True)
        h0, h1, h2 = mask & 1, (mask >> 1) & 1, (mask >> 2) & 1
        first = jnp.where(h0 == 1, 0, jnp.where(h1 == 1, 1, jnp.where(h2 == 1, 2, 3)))
        second = jnp.where(h0 + h1 == 2, 1, jnp.where((h0 + h1 == 1) & (h2 == 1), 2, 3))
        pick[0, pl.ds(8 * p, 8), :] = jnp.broadcast_to(first, (8, HD))
        pick[1, pl.ds(8 * p, 8), :] = jnp.broadcast_to(second, (8, HD))
    source = lax.broadcasted_iota(jnp.int32, (SOURCES, 256), 0)
    lane_16 = lax.broadcasted_iota(jnp.int32, (SOURCES, 256), 1)
    sx, sy = source >> 3, (source >> 2) & 1
    sz, sc = (source >> 1) & 1, source & 1
    for t in range(SLOTS):
        u, v = t // 2, t % 2
        ax, ay, az = (u + y) % 2, (v + z) % 2, (u + v + x) % 2
        nx = (x + 5 - 2 * ((x + ax) % 2)) % 4
        ny = (y + 5 - 2 * ((y + ay) % 2)) % 4
        nz = (z + 5 - 2 * ((z + az) % 2)) % 4
        fx = jnp.where(sx == 0, x, nx)
        fy = jnp.where(sy == 0, y, ny)
        fz = jnp.where(sz == 0, z, nz)
        fc = jnp.where(sc == 0, c, 1 - c)
        owner = (fz * 2 + fc) * 16 + fx * 4 + fy
        p_ = 2 * (2 * u + z % 2) + c
        h_ = 2 * (2 * v + x % 2) + (y + u + v) % 2
        row = kept_ref[p_, pl.ds(h_, 1), :]
        counts = jnp.where(lane_8 == h_, counts_ref[pl.ds(p_, 1), :], 0)
        live = lane_16 < jnp.sum(counts, axis=1, keepdims=True)
        here = jnp.where(live & ((row >> 2) == owner), 1, 0)
        live_keys[pl.ds(16 * t, 16), :] = jnp.broadcast_to(
            BLOCK * jnp.sum(here, axis=1, keepdims=True), (SOURCES, 2 * GROUP)
        )

    def pack(t, cls, dst):
        u, v = t // 2, t % 2
        rx = (x + cls // 8) % 2
        ry = (y + cls // 4) % 2
        rz = (z + cls // 2) % 2
        rc = (c + cls) % 2
        p_loc = 2 * rz + rc
        h_loc = 2 * rx + (ry + u + v) % 2
        pair = (4 * u + p_loc) * 8 + 4 * v + h_loc
        columns = pl.ds(pl.multiple_of(h_loc * HD, HD), HD)
        for slot in range(CAP):
            chosen = jnp.broadcast_to(pick[slot, pl.ds(pair, 1), :], (16, HD))
            part = [None, None]
            for block in range(slot, 4):
                weight = jnp.where(chosen == block, 1.0, 0.0).astype(jnp.bfloat16)
                weight = jnp.concatenate([weight] * (BLOCK // 16), axis=0)
                for kind in range(2):
                    rows = kv_buf[t, kind, p_loc, pl.ds(block * BLOCK, BLOCK), columns] * weight
                    part[kind] = rows if part[kind] is None else part[kind] + rows
            for kind in range(2):
                dst[kind, pl.ds(slot * BLOCK, BLOCK), :] = part[kind]

    def pack_slot(t):
        kv_copy(t).wait()
        pack(t, 0, recv.at[t, 0])

        def one(cls, carry):
            pack(t, cls, packed.at[t * 15 + cls - 1])
            return carry

        lax.fori_loop(1, SOURCES, one, 0)

    def send_slot(t):
        u, v = t // 2, t % 2

        def one(i, carry):
            cls = (i * 5) % 16
            dx, dy, dz, dc = cls // 8, (cls // 4) % 2, (cls // 2) % 2, cls % 2
            rx, ry, rz, rc = (x + dx) % 2, (y + dy) % 2, (z + dz) % 2, (c + dc) % 2
            ax, ay, az = (u + ry) % 2, (v + rz) % 2, (u + v + rx) % 2
            x_ = (x + dx * (1 - 2 * ((x + ax) % 2)) + 4) % 4
            y_ = (y + dy * (1 - 2 * ((y + ay) % 2)) + 4) % 4
            z_ = (z + dz * (1 - 2 * ((z + az) % 2)) + 4) % 4
            pltpu.make_async_remote_copy(
                src_ref=packed.at[t * 15 + cls - 1],
                dst_ref=recv.at[t, cls],
                send_sem=pack_sem,
                recv_sem=recv_sem.at[t],
                device_id=device(x_, y_, z_, rc),
                device_id_type=MESH,
            ).start()
            return carry

        lax.fori_loop(1, SOURCES, one, 0)

    pack_slot(0)
    pl.semaphore_wait(barrier, 68)
    send_slot(0)
    pack_slot(1)
    send_slot(1)

    tok_copy.wait()

    def norm(i, carry):
        rows = pl.ds(pl.multiple_of(i * 16, 16), 16)
        values = tok[rows, :].astype(jnp.float32)
        mean_square = jnp.mean(values * values, axis=-1, keepdims=True)
        normed[rows, :] = (values * lax.rsqrt(mean_square + 1e-05) * gain_ref[...]).astype(
            jnp.bfloat16
        )
        return carry

    lax.fori_loop(0, STEPS // 16, norm, 0)
    wk_copy.wait()
    wv_copy.wait()
    n_acc[...] = jnp.zeros_like(n_acc)
    q_acc[...] = jnp.zeros_like(q_acc)

    def project(k, carry):
        columns = pl.ds(pl.multiple_of(k * CHUNK, CHUNK), CHUNK)
        wq_copy(k).wait()
        rows = normed[:, columns]
        q_acc[...] += jnp.dot(rows, wq[columns, :], preferred_element_type=jnp.float32)
        n_acc[...] += lax.dot_general(rows, wkv[:, columns], NT, preferred_element_type=jnp.float32)
        return carry

    lax.fori_loop(0, CHUNKS, project, 0)

    mine = n_acc[...].astype(jnp.bfloat16)
    piece[...] = mine
    piece_copy = pltpu.make_async_remote_copy(
        src_ref=piece,
        dst_ref=other,
        send_sem=piece_sem.at[0],
        recv_sem=piece_sem.at[1],
        device_id=device(x, y + 1 - 2 * (y % 2), z, c),
        device_id_type=MESH,
    )
    piece_copy.start()
    for g in range(4):
        q_send[pl.ds(g * STEPS, STEPS), :] = q_acc[:, g * HD : (g + 1) * HD].astype(jnp.bfloat16)
    half = y % 2
    home_slot = 2 * (z // 2) + x // 2
    home_parity = (y // 2 + z // 2 + x // 2) % 2
    stays = half == home_parity

    def q_copy(i):
        bx, by, bz = i // 4, (i // 2) % 2, i % 2
        return pltpu.make_async_remote_copy(
            src_ref=q_send,
            dst_ref=q_buf.at[home_slot, half],
            send_sem=q_send_sem.at[i],
            recv_sem=q_recv_sem.at[home_slot, half],
            device_id=device((x + 2 * bx) % 4, home_parity + 2 * by, (z + 2 * bz) % 4, c),
            device_id_type=MESH,
        )

    def is_self(i):
        return (i // 4 == 0) & (i % 2 == 0) & (home_parity + 2 * ((i // 2) % 2) == y)

    def q_start(i, carry):
        @pl.when(jnp.logical_not(is_self(i)))
        def _():
            q_copy(i).start()

        @pl.when(is_self(i))
        def _():
            q_buf[home_slot, half] = q_send[...]

        return carry

    lax.fori_loop(0, SITES, q_start, 0)

    for t in range(2, SLOTS):
        pack_slot(t)
        send_slot(t)

    piece_copy.wait()
    mine = piece[...].astype(jnp.float32)
    theirs = other[...].astype(jnp.float32)
    low = jnp.where(half == 0, mine, theirs)
    high = jnp.where(half == 0, theirs, mine)
    first_half = lax.broadcasted_iota(jnp.int32, (STEPS, HD), 1) < 64
    new_keys = jnp.where(first_half, low, pltpu.roll(high, 64, 1)).astype(jnp.bfloat16)
    new_values = jnp.where(first_half, pltpu.roll(low, 64, 1), high).astype(jnp.bfloat16)
    ent_ref[pl.ds(0, STEPS), :] = new_keys
    ent_ref[pl.ds(STEPS, STEPS), :] = new_values
    scores = lax.dot_general(new_keys, q_send[...], NT, preferred_element_type=jnp.float32)
    key_step = lax.broadcasted_iota(jnp.int32, (STEPS, GROUP), 0)
    row_step = lax.broadcasted_iota(jnp.int32, (STEPS, GROUP), 1) % STEPS
    scores = jnp.where(key_step <= row_step, scores, LOWEST)
    top = jnp.max(scores, axis=0, keepdims=True)
    weights = jnp.exp2((scores - top) * EXP_SCALE)
    own_l[...] = jnp.broadcast_to(
        top * EXP_SCALE + jnp.log2(jnp.sum(weights, axis=0, keepdims=True)), (8, GROUP)
    )
    own_o[...] = lax.dot_general(
        new_values, weights.astype(jnp.bfloat16), TN, preferred_element_type=jnp.float32
    ) / jnp.sum(weights, axis=0, keepdims=True)

    key_row = lax.broadcasted_iota(jnp.int32, (KEYS, 2 * GROUP), 0)

    def home_of(t):
        u, v = t // 2, t % 2
        x0, z0 = 2 * v + x % 2, 2 * u + z % 2
        hlo = (y + u + v) % 2
        near = (x0 == x) & (z0 == z) & (hlo == y // 2)
        bx, bz = (x + 4 - x0) // 2 % 2, (z + 4 - z0) // 2 % 2
        return x0, z0, hlo, near, bx * 4 + (y // 2) * 2 + bz

    def out_copies(t, m):
        x0, z0, hlo, _, site = home_of(t)
        home = device(x0, 2 * hlo + m, z0, c)
        return (
            pltpu.make_async_remote_copy(
                src_ref=o_send.at[t, m],
                dst_ref=o_buf.at[site],
                send_sem=o_send_sem.at[t, m],
                recv_sem=o_recv_sem.at[site],
                device_id=home,
                device_id_type=MESH,
            ),
            pltpu.make_async_remote_copy(
                src_ref=l_send.at[t, m],
                dst_ref=l_buf.at[site],
                send_sem=l_send_sem.at[t, m],
                recv_sem=l_recv_sem.at[site],
                device_id=home,
                device_id_type=MESH,
            ),
        )

    def attend(t, carry):
        x0, z0, hlo, near, site = home_of(t)
        for m in range(2):

            @pl.when(jnp.logical_not(near & (y % 2 == m)))
            def _(m=m):
                pltpu.make_async_copy(
                    q_buf.at[t, m], q_buf.at[t, m], q_recv_sem.at[t, m]
                ).wait()

        arrived = recv.at[t, pl.ds(1, SOURCES - 1)]
        pltpu.make_async_copy(arrived, arrived, recv_sem.at[t]).wait()
        q = q_buf[t].reshape(2 * GROUP, HD)

        keys = recv[t, :, 0].reshape(SOURCES * KEYS, HD)
        values = recv[t, :, 1].reshape(SOURCES * KEYS, HD)
        s = lax.dot_general(keys, q, NT, preferred_element_type=jnp.float32)
        s = jnp.concatenate(
            [
                jnp.where(
                    key_row < live_keys[pl.ds(16 * t + i, 1), :],
                    s[i * KEYS : (i + 1) * KEYS],
                    LOWEST,
                )
                for i in range(SOURCES)
            ],
            axis=0,
        )
        top = jnp.max(s, axis=0, keepdims=True)
        w = jnp.exp2((s - top) * EXP_SCALE)
        total = jnp.sum(w, axis=0, keepdims=True)
        o = lax.dot_general(
            values, w.astype(jnp.bfloat16), TN, preferred_element_type=jnp.float32
        )
        o = (o / total).astype(jnp.bfloat16)
        lse = jnp.broadcast_to(top * EXP_SCALE + jnp.log2(total), (8, 2 * GROUP))
        for m in range(2):
            o_send[t, m] = o[:, m * GROUP : (m + 1) * GROUP]
            l_send[t, m] = lse[:, m * GROUP : (m + 1) * GROUP]
            leaves = jnp.logical_not(near & (y % 2 == m))

            @pl.when(leaves)
            def _(m=m):
                for copy in out_copies(t, m):
                    copy.start()

            @pl.when(jnp.logical_not(leaves))
            def _(m=m):
                o_buf[site] = o_send[t, m]
                l_buf[site] = l_send[t, m]

        return carry

    lax.fori_loop(0, SLOTS, attend, 0)

    def await_site(i, carry):
        @pl.when(jnp.logical_not(is_self(i)))
        def _():
            pltpu.make_async_copy(o_buf.at[i], o_buf.at[i], o_recv_sem.at[i]).wait()
            pltpu.make_async_copy(l_buf.at[i], l_buf.at[i], l_recv_sem.at[i]).wait()

        return carry

    lax.fori_loop(0, SITES, await_site, 0)
    top = own_l[pl.ds(0, 1), :]
    for i in range(SITES):
        top = jnp.maximum(top, l_buf[i, pl.ds(0, 1), :])
    share = jnp.exp2(own_l[pl.ds(0, 1), :] - top)
    total = share
    result = own_o[...] * share
    for i in range(SITES):
        share = jnp.exp2(l_buf[i, pl.ds(0, 1), :] - top)
        total = total + share
        result = result + o_buf[i].astype(jnp.float32) * share
    result = (result / total).T
    for g in range(4):
        att_ref[:, g * HD : (g + 1) * HD] = result[g * STEPS : (g + 1) * STEPS, :].astype(
            jnp.bfloat16
        )

    pltpu.make_async_copy(packed, packed, pack_sem).wait()

    def await_q(i, carry):
        @pl.when(jnp.logical_not(is_self(i)))
        def _():
            q_copy(i).wait_send()

        return carry

    lax.fori_loop(0, SITES, await_q, 0)

    def await_out(t, carry):
        _, _, _, near, _ = home_of(t)
        for m in range(2):

            @pl.when(jnp.logical_not(near & (y % 2 == m)))
            def _(m=m):
                for copy in out_copies(t, m):
                    copy.wait_send()

        return carry

    lax.fori_loop(0, SLOTS, await_out, 0)


def per_device(
    new_tokens,
    norm_gain,
    query_weight,
    key_weight,
    value_weight,
    kv_cache,
    kept_blocks,
    kept_counts,
):
    vmem = pl.BlockSpec(memory_space=pltpu.VMEM)
    hbm = pl.BlockSpec(memory_space=pl.ANY)
    bf16, f32 = jnp.bfloat16, jnp.float32
    dma = pltpu.SemaphoreType.DMA
    attended, entries = pl.pallas_call(
        kernel,
        out_shape=(
            jax.ShapeDtypeStruct((STEPS, 4 * HD), bf16),
            jax.ShapeDtypeStruct((2 * STEPS, HD), bf16),
        ),
        in_specs=[hbm, vmem, hbm, hbm, hbm, hbm, vmem, vmem],
        out_specs=(vmem, vmem),
        scratch_shapes=[
            pltpu.VMEM((SLOTS, 2, 4, TOKD, 4 * HD), bf16),
            pltpu.VMEM((SLOTS * (SOURCES - 1), 2, KEYS, HD), bf16),
            pltpu.VMEM((SLOTS, SOURCES, 2, KEYS, HD), bf16),
            pltpu.VMEM((STEPS, WIDTH), bf16),
            pltpu.VMEM((STEPS, WIDTH), bf16),
            pltpu.VMEM((WIDTH, 4 * HD), bf16),
            pltpu.VMEM((HD, WIDTH), bf16),
            pltpu.VMEM((STEPS, 4 * HD), f32),
            pltpu.VMEM((STEPS, HD), f32),
            pltpu.VMEM((GROUP, HD), bf16),
            pltpu.VMEM((SLOTS, 2, GROUP, HD), bf16),
            pltpu.VMEM((CAP, 64, HD), jnp.int32),
            pltpu.VMEM((SLOTS * SOURCES, 2 * GROUP), jnp.int32),
            pltpu.VMEM((SLOTS, 2, HD, GROUP), bf16),
            pltpu.VMEM((SLOTS, 2, 8, GROUP), f32),
            pltpu.VMEM((SITES, HD, GROUP), bf16),
            pltpu.VMEM((SITES, 8, GROUP), f32),
            pltpu.VMEM((HD, GROUP), f32),
            pltpu.VMEM((8, GROUP), f32),
            pltpu.VMEM((STEPS, HD), bf16),
            pltpu.VMEM((STEPS, HD), bf16),
            dma((SLOTS,)),
            dma((CHUNKS + 2,)),
            dma,
            dma,
            dma((SLOTS,)),
            dma((SITES,)),
            dma((SLOTS, 2)),
            dma((SLOTS, 2)),
            dma((SITES,)),
            dma((SLOTS, 2)),
            dma((SITES,)),
            dma((2,)),
        ],
        compiler_params=pltpu.CompilerParams(
            collective_id=0, has_side_effects=True, vmem_limit_bytes=56 * 1024 * 1024
        ),
    )(
        new_tokens.reshape(STEPS, WIDTH),
        norm_gain.reshape(1, WIDTH),
        query_weight,
        key_weight.T,
        value_weight.T,
        kv_cache,
        kept_blocks,
        kept_counts,
    )
    return (
        attended.reshape(STEPS, 1, 4 * HD),
        entries.reshape(1, 1, 2 * STEPS * HD),
    )


def solution(mesh):
    in_specs = (
        P(None, "seq", None),
        P(),
        P(None, "tp"),
        P(None, "tp"),
        P(None, "tp"),
        P(None, None, ("seq", "tp"), None),
        P(),
        P(),
    )
    out_specs = (P(None, "seq", "tp"), P("seq", "tp", None))
    return jax.shard_map(
        per_device, mesh=mesh, in_specs=in_specs, out_specs=out_specs, check_vma=False
    )
```

```python
import math

import jax
import jax.numpy as jnp
from jax import lax
from jax.experimental import pallas as pl
from jax.experimental.pallas import tpu as pltpu
from jax.sharding import PartitionSpec as P

HD = 128
BLOCK = 64
CAP = 2
STEPS = 64
KEYS = CAP * BLOCK
TOKD = 256
WIDTH = 8192
SLOTS = 4
SOURCES = 16
SITES = 8
GROUP = 256
CHUNKS = 8
CHUNK = WIDTH // CHUNKS
MESH = pl.DeviceIdType.MESH
EXP_SCALE = math.log2(math.e) / math.sqrt(HD)
LOWEST = -1e30

NT = (((1,), (1,)), ((), ()))
TN = (((0,), (0,)), ((), ()))


def kernel(
    tok_hbm,
    gain_hbm,
    wq_hbm,
    wk_hbm,
    wv_hbm,
    kv_hbm,
    kept_hbm,
    counts_hbm,
    att_ref,
    ent_ref,
    gain_ref,
    kept_ref,
    counts_ref,
    kv_buf,
    packed,
    recv,
    tok,
    normed,
    wq,
    wkv,
    q_acc,
    n_acc,
    q_send,
    q_buf,
    pick,
    live_keys,
    o_send,
    l_send,
    o_buf,
    l_buf,
    own_o,
    own_l,
    piece,
    other,
    kv_sem,
    w_sem,
    tok_sem,
    small_sem,
    pack_sem,
    recv_sem,
    q_send_sem,
    q_recv_sem,
    o_send_sem,
    o_recv_sem,
    l_send_sem,
    l_recv_sem,
    piece_sem,
):
    seq = lax.axis_index("seq")
    tp = lax.axis_index("tp")
    z, c = seq // 2, seq % 2
    x, y = tp // 4, tp % 4
    flat = seq * 16 + tp

    def device(x_, y_, z_, c_):
        return (z_ * 2 + c_, x_ * 4 + y_)

    def other_y(y_, odd):
        return (y_ + 1 - 2 * ((y_ + 1 + odd) % 2) + 4) % 4

    def pair_at(x_, y_, z_, c_, u, v):
        g = 1 - 2 * c_
        x0, z0 = (x_ - v * g + 4) % 4, (z_ - u * g + 4) % 4
        row = (y_ + ((x0 + z0) % 2) * (1 + 2 * c_)) % 4
        return x0, z0, row // 2, row % 2

    def kv_start(t):
        u, v = t // 2, t % 2
        for part in range(8):
            dc, dz, dx = part // 4, (part // 2) % 2, part % 2
            c_ = (c + dc) % 2
            g = 1 - 2 * c_
            x0 = (x - dx * g * (2 * v - 1) - v * g + 8) % 4
            z0 = (z - dz * g * (2 * u - 1) - u * g + 8) % 4
            pltpu.make_async_copy(
                kv_hbm.at[:, 2 * z0 + c_, :, pl.ds(pl.multiple_of(x0 * 2 * HD, 2 * HD), 2 * HD)],
                kv_buf.at[t, part],
                kv_sem.at[t],
            ).start()

    def wq_copy(k):
        rows = pl.ds(pl.multiple_of(k * CHUNK, CHUNK), CHUNK)
        return pltpu.make_async_copy(wq_hbm.at[rows], wq.at[rows], w_sem.at[k])

    tok_copy = pltpu.make_async_copy(tok_hbm, tok, tok_sem)
    wk_copy = pltpu.make_async_copy(wk_hbm, wkv.at[pl.ds(0, 64)], w_sem.at[CHUNKS])
    wv_copy = pltpu.make_async_copy(wv_hbm, wkv.at[pl.ds(64, 64)], w_sem.at[CHUNKS + 1])
    gain_copy = pltpu.make_async_copy(gain_hbm, gain_ref, small_sem.at[0])
    kept_copy = pltpu.make_async_copy(kept_hbm, kept_ref, small_sem.at[1])
    counts_copy = pltpu.make_async_copy(counts_hbm, counts_ref, small_sem.at[2])
    kept_copy.start()
    counts_copy.start()
    kv_start(3)
    kv_start(2)
    gain_copy.start()

    barrier = pltpu.get_barrier_semaphore()

    def greet_near(i, carry):
        c_ = (c + i) % 2
        z_ = (z + (i // 2) % 3 + 3) % 4
        y_ = (y + (i // 6) % 3 + 3) % 4
        x_ = (x + i // 18 + 3) % 4

        @pl.when(i != 26)
        def _():
            pl.semaphore_signal(
                barrier, inc=1, device_id=device(x_, y_, z_, c_), device_id_type=MESH
            )

        return carry

    lax.fori_loop(0, 54, greet_near, 0)

    def greet_far(i, carry):
        z_ = (z + i % 3 + 3) % 4
        x_ = (x + i // 3 + 3) % 4
        pl.semaphore_signal(
            barrier, inc=1, device_id=device(x_, (y + 2) % 4, z_, c), device_id_type=MESH
        )
        return carry

    lax.fori_loop(0, 9, greet_far, 0)

    kept_copy.wait()
    counts_copy.wait()
    lane = lax.broadcasted_iota(jnp.int32, (8, 256), 1)
    eye = lax.broadcasted_iota(jnp.int32, (8, 8), 0) == lax.broadcasted_iota(jnp.int32, (8, 8), 1)
    lane_8 = lax.broadcasted_iota(jnp.int32, (1, 8), 1)
    for p in range(8):
        count = jnp.sum(jnp.where(eye, counts_ref[pl.ds(p, 1), :], 0), axis=1, keepdims=True)
        rel = kept_ref[p] - 4 * flat
        code = jnp.where(rel == 0, 1, jnp.where(rel == 1, 2, jnp.where(rel == 2, 4, 8)))
        code = jnp.where((rel >= 0) & (rel < 4) & (lane < count), code, 0)
        mask = jnp.sum(code, axis=1, keepdims=True)
        h0, h1, h2 = mask & 1, (mask >> 1) & 1, (mask >> 2) & 1
        first = jnp.where(h0 == 1, 0, jnp.where(h1 == 1, 1, jnp.where(h2 == 1, 2, 3)))
        second = jnp.where(h0 + h1 == 2, 1, jnp.where((h0 + h1 == 1) & (h2 == 1), 2, 3))
        pick[0, pl.ds(8 * p, 8), :] = jnp.broadcast_to(first, (8, HD))
        pick[1, pl.ds(8 * p, 8), :] = jnp.broadcast_to(second, (8, HD))
    source = lax.broadcasted_iota(jnp.int32, (SOURCES, 256), 0)
    lane_16 = lax.broadcasted_iota(jnp.int32, (SOURCES, 256), 1)
    sx, sy = source >> 3, (source >> 2) & 1
    sz, sc = (source >> 1) & 1, source & 1
    for t in range(SLOTS):
        u, v = t // 2, t % 2
        g = 1 - 2 * c
        x0, z0, hlo, _ = pair_at(x, y, z, c, u, v)
        nx = (x + g * (2 * v - 1) + 4) % 4
        nz = (z + g * (2 * u - 1) + 4) % 4
        ny = other_y(y, (x0 + z0) % 2)
        fx = jnp.where(sx == 0, x, nx)
        fy = jnp.where(sy == 0, y, ny)
        fz = jnp.where(sz == 0, z, nz)
        fc = jnp.where(sc == 0, c, 1 - c)
        owner = (fz * 2 + fc) * 16 + fx * 4 + fy
        p_, h_ = 2 * z0 + c, 2 * x0 + hlo
        row = kept_ref[p_, pl.ds(h_, 1), :]
        counts = jnp.where(lane_8 == h_, counts_ref[pl.ds(p_, 1), :], 0)
        live = lane_16 < jnp.sum(counts, axis=1, keepdims=True)
        here = jnp.where(live & ((row >> 2) == owner), 1, 0)
        live_keys[pl.ds(16 * t, 16), :] = jnp.broadcast_to(
            BLOCK * jnp.sum(here, axis=1, keepdims=True), (SOURCES, 2 * GROUP)
        )

    def site_of(t, cls):
        u, v = t // 2, t % 2
        dx, dy, dz, c_ = cls // 8, (cls // 4) % 2, (cls // 2) % 2, (c + cls) % 2
        g = 1 - 2 * c_
        x_ = (x - dx * g * (2 * v - 1) + 4) % 4
        z_ = (z - dz * g * (2 * u - 1) + 4) % 4
        odd = (x_ + z_ + u + v) % 2
        y_ = y + dy * (other_y(y, odd) - y)
        return x_, y_, z_, c_

    def pack(t, cls, dst):
        x_, y_, z_, c_ = site_of(t, cls)
        x0, z0, hlo, _ = pair_at(x_, y_, z_, c_, t // 2, t % 2)
        part = (cls % 2) * 4 + ((cls // 2) % 2) * 2 + cls // 8
        pair = (2 * z0 + c_) * 8 + 2 * x0 + hlo
        columns = pl.ds(pl.multiple_of(hlo * HD, HD), HD)
        for slot in range(CAP):
            chosen = jnp.broadcast_to(pick[slot, pl.ds(pair, 1), :], (16, HD))
            total = [None, None]
            for block in range(slot, 4):
                weight = jnp.where(chosen == block, 1.0, 0.0).astype(jnp.bfloat16)
                weight = jnp.concatenate([weight] * (BLOCK // 16), axis=0)
                for kind in range(2):
                    rows = kv_buf[t, part, kind, pl.ds(block * BLOCK, BLOCK), columns] * weight
                    total[kind] = rows if total[kind] is None else total[kind] + rows
            for kind in range(2):
                dst[kind, pl.ds(slot * BLOCK, BLOCK), :] = total[kind]

    def pack_slot(t):
        pltpu.make_async_copy(kv_buf.at[t], kv_buf.at[t], kv_sem.at[t]).wait()

        def one(cls, carry):
            pack(t, cls, packed.at[t * 15 + cls - 1])
            return carry

        lax.fori_loop(1, SOURCES, one, 0)

    def send_slot(t):
        def one(i, carry):
            cls = (i * 5) % 16
            pltpu.make_async_remote_copy(
                src_ref=packed.at[t * 15 + cls - 1],
                dst_ref=recv.at[t, cls],
                send_sem=pack_sem,
                recv_sem=recv_sem.at[t],
                device_id=device(*site_of(t, cls)),
                device_id_type=MESH,
            ).start()
            return carry

        lax.fori_loop(1, SOURCES, one, 0)

    pack_slot(3)
    pl.semaphore_wait(barrier, 62)
    send_slot(3)
    tok_copy.start()
    wk_copy.start()
    wv_copy.start()
    for k in range(CHUNKS):
        wq_copy(k).start()
    kv_start(1)
    kv_start(0)
    pack_slot(2)
    send_slot(2)

    tok_copy.wait()
    gain_copy.wait()

    def norm(i, carry):
        rows = pl.ds(pl.multiple_of(i * 16, 16), 16)
        values = tok[rows, :].astype(jnp.float32)
        mean_square = jnp.mean(values * values, axis=-1, keepdims=True)
        normed[rows, :] = (values * lax.rsqrt(mean_square + 1e-05) * gain_ref[...]).astype(
            jnp.bfloat16
        )
        return carry

    lax.fori_loop(0, STEPS // 16, norm, 0)
    wk_copy.wait()
    wv_copy.wait()
    n_acc[...] = jnp.zeros_like(n_acc)
    q_acc[...] = jnp.zeros_like(q_acc)

    def project(k, carry):
        columns = pl.ds(pl.multiple_of(k * CHUNK, CHUNK), CHUNK)
        wq_copy(k).wait()
        rows = normed[:, columns]
        q_acc[...] += jnp.dot(rows, wq[columns, :], preferred_element_type=jnp.float32)
        n_acc[...] += lax.dot_general(rows, wkv[:, columns], NT, preferred_element_type=jnp.float32)
        return carry

    lax.fori_loop(0, CHUNKS, project, 0)

    mine = n_acc[...].astype(jnp.bfloat16)
    piece[...] = mine
    piece_copy = pltpu.make_async_remote_copy(
        src_ref=piece,
        dst_ref=other,
        send_sem=piece_sem.at[0],
        recv_sem=piece_sem.at[1],
        device_id=device(x, y + 1 - 2 * (y % 2), z, c),
        device_id_type=MESH,
    )
    piece_copy.start()
    for g in range(4):
        q_send[pl.ds(g * STEPS, STEPS), :] = q_acc[:, g * HD : (g + 1) * HD].astype(jnp.bfloat16)
    half = y % 2
    toward = 1 - 2 * c
    shift = ((x + z) % 2) * (1 + 2 * c)

    def site_y(i):
        return (2 * (y // 2) + (i // 2) % 2 - shift + 4) % 4

    def q_copy(i):
        bx, bz = i // 4, i % 2
        return pltpu.make_async_remote_copy(
            src_ref=q_send,
            dst_ref=q_buf.at[2 * bz + bx, half],
            send_sem=q_send_sem.at[i],
            recv_sem=q_recv_sem.at[2 * bz + bx, half],
            device_id=device(
                (x + bx * toward + 4) % 4, site_y(i), (z + bz * toward + 4) % 4, c
            ),
            device_id_type=MESH,
        )

    def is_self(i):
        return (i // 4 == 0) & (i % 2 == 0) & (site_y(i) == y)

    def q_start(i, carry):
        @pl.when(jnp.logical_not(is_self(i)))
        def _():
            q_copy(i).start()

        @pl.when(is_self(i))
        def _():
            q_buf[0, half] = q_send[...]

        return carry

    lax.fori_loop(0, SITES, q_start, 0)

    for t in (1, 0):
        pack_slot(t)
        send_slot(t)

    piece_copy.wait()
    mine = piece[...].astype(jnp.float32)
    theirs = other[...].astype(jnp.float32)
    low = jnp.where(half == 0, mine, theirs)
    high = jnp.where(half == 0, theirs, mine)
    first_half = lax.broadcasted_iota(jnp.int32, (STEPS, HD), 1) < 64
    new_keys = jnp.where(first_half, low, pltpu.roll(high, 64, 1)).astype(jnp.bfloat16)
    new_values = jnp.where(first_half, pltpu.roll(low, 64, 1), high).astype(jnp.bfloat16)
    ent_ref[pl.ds(0, STEPS), :] = new_keys
    ent_ref[pl.ds(STEPS, STEPS), :] = new_values
    scores = lax.dot_general(new_keys, q_send[...], NT, preferred_element_type=jnp.float32)
    key_step = lax.broadcasted_iota(jnp.int32, (STEPS, GROUP), 0)
    row_step = lax.broadcasted_iota(jnp.int32, (STEPS, GROUP), 1) % STEPS
    scores = jnp.where(key_step <= row_step, scores, LOWEST)
    top = jnp.max(scores, axis=0, keepdims=True)
    weights = jnp.exp2((scores - top) * EXP_SCALE)
    own_l[...] = jnp.broadcast_to(
        top * EXP_SCALE + jnp.log2(jnp.sum(weights, axis=0, keepdims=True)), (8, GROUP)
    )
    own_o[...] = lax.dot_general(
        new_values, weights.astype(jnp.bfloat16), TN, preferred_element_type=jnp.float32
    ) / jnp.sum(weights, axis=0, keepdims=True)

    key_row = lax.broadcasted_iota(jnp.int32, (KEYS, 2 * GROUP), 0)

    def home_of(t):
        u, v = t // 2, t % 2
        x0, z0, hlo, by = pair_at(x, y, z, c, u, v)
        near = (t == 0) & (hlo == y // 2)
        return x0, z0, hlo, near, v * 4 + by * 2 + u

    def out_copies(t, m):
        x0, z0, hlo, _, site = home_of(t)
        home = device(x0, 2 * hlo + m, z0, c)
        return (
            pltpu.make_async_remote_copy(
                src_ref=o_send.at[t, m],
                dst_ref=o_buf.at[site],
                send_sem=o_send_sem.at[t, m],
                recv_sem=o_recv_sem.at[site],
                device_id=home,
                device_id_type=MESH,
            ),
            pltpu.make_async_remote_copy(
                src_ref=l_send.at[t, m],
                dst_ref=l_buf.at[site],
                send_sem=l_send_sem.at[t, m],
                recv_sem=l_recv_sem.at[site],
                device_id=home,
                device_id_type=MESH,
            ),
        )

    def attend(step, carry):
        t = SLOTS - 1 - step
        x0, z0, hlo, near, site = home_of(t)
        for m in range(2):

            @pl.when(jnp.logical_not(near & (y % 2 == m)))
            def _(m=m):
                pltpu.make_async_copy(
                    q_buf.at[t, m], q_buf.at[t, m], q_recv_sem.at[t, m]
                ).wait()

        arrived = recv.at[t, pl.ds(1, SOURCES - 1)]
        pltpu.make_async_copy(arrived, arrived, recv_sem.at[t]).wait()
        pack(t, 0, recv.at[t, 0])
        q = q_buf[t].reshape(2 * GROUP, HD)

        keys = recv[t, :, 0].reshape(SOURCES * KEYS, HD)
        values = recv[t, :, 1].reshape(SOURCES * KEYS, HD)
        s = lax.dot_general(keys, q, NT, preferred_element_type=jnp.float32)
        s = jnp.concatenate(
            [
                jnp.where(
                    key_row < live_keys[pl.ds(16 * t + i, 1), :],
                    s[i * KEYS : (i + 1) * KEYS],
                    LOWEST,
                )
                for i in range(SOURCES)
            ],
            axis=0,
        )
        top = jnp.max(s, axis=0, keepdims=True)
        w = jnp.exp2((s - top) * EXP_SCALE)
        total = jnp.sum(w, axis=0, keepdims=True)
        o = lax.dot_general(
            values, w.astype(jnp.bfloat16), TN, preferred_element_type=jnp.float32
        )
        o = (o / total).astype(jnp.bfloat16)
        lse = jnp.broadcast_to(top * EXP_SCALE + jnp.log2(total), (8, 2 * GROUP))
        for m in range(2):
            o_send[t, m] = o[:, m * GROUP : (m + 1) * GROUP]
            l_send[t, m] = lse[:, m * GROUP : (m + 1) * GROUP]
            leaves = jnp.logical_not(near & (y % 2 == m))

            @pl.when(leaves)
            def _(m=m):
                for copy in out_copies(t, m):
                    copy.start()

            @pl.when(jnp.logical_not(leaves))
            def _(m=m):
                o_buf[site] = o_send[t, m]
                l_buf[site] = l_send[t, m]

        return carry

    lax.fori_loop(0, SLOTS, attend, 0)

    def await_site(i, carry):
        @pl.when(jnp.logical_not(is_self(i)))
        def _():
            pltpu.make_async_copy(o_buf.at[i], o_buf.at[i], o_recv_sem.at[i]).wait()
            pltpu.make_async_copy(l_buf.at[i], l_buf.at[i], l_recv_sem.at[i]).wait()

        return carry

    lax.fori_loop(0, SITES, await_site, 0)
    top = own_l[pl.ds(0, 1), :]
    for i in range(SITES):
        top = jnp.maximum(top, l_buf[i, pl.ds(0, 1), :])
    share = jnp.exp2(own_l[pl.ds(0, 1), :] - top)
    total = share
    result = own_o[...] * share
    for i in range(SITES):
        share = jnp.exp2(l_buf[i, pl.ds(0, 1), :] - top)
        total = total + share
        result = result + o_buf[i].astype(jnp.float32) * share
    result = (result / total).T
    for g in range(4):
        att_ref[:, g * HD : (g + 1) * HD] = result[g * STEPS : (g + 1) * STEPS, :].astype(
            jnp.bfloat16
        )

    pltpu.make_async_copy(packed, packed, pack_sem).wait()

    def await_q(i, carry):
        @pl.when(jnp.logical_not(is_self(i)))
        def _():
            q_copy(i).wait_send()

        return carry

    lax.fori_loop(0, SITES, await_q, 0)

    def await_out(t, carry):
        _, _, _, near, _ = home_of(t)
        for m in range(2):

            @pl.when(jnp.logical_not(near & (y % 2 == m)))
            def _(m=m):
                for copy in out_copies(t, m):
                    copy.wait_send()

        return carry

    lax.fori_loop(0, SLOTS, await_out, 0)


def place(att_ref, ent_ref, att_out, ent_out):
    att_out[...] = att_ref[...]
    for row in range(2 * STEPS):
        ent_out[0, :, row * HD : (row + 1) * HD] = ent_ref[row : row + 1, :]


def per_device(
    new_tokens,
    norm_gain,
    query_weight,
    key_weight,
    value_weight,
    kv_cache,
    kept_blocks,
    kept_counts,
):
    vmem = pl.BlockSpec(memory_space=pltpu.VMEM)
    hbm = pl.BlockSpec(memory_space=pl.ANY)
    bf16, f32 = jnp.bfloat16, jnp.float32
    dma = pltpu.SemaphoreType.DMA
    attended, entries = pl.pallas_call(
        kernel,
        out_shape=(
            jax.ShapeDtypeStruct((STEPS, 4 * HD), bf16),
            jax.ShapeDtypeStruct((2 * STEPS, HD), bf16),
        ),
        in_specs=[hbm] * 8,
        out_specs=(vmem, vmem),
        scratch_shapes=[
            pltpu.VMEM((1, WIDTH), f32),
            pltpu.VMEM((8, 8, 256), jnp.int32),
            pltpu.VMEM((8, 8), jnp.int32),
            pltpu.VMEM((SLOTS, 8, 2, TOKD, 2 * HD), bf16),
            pltpu.VMEM((SLOTS * (SOURCES - 1), 2, KEYS, HD), bf16),
            pltpu.VMEM((SLOTS, SOURCES, 2, KEYS, HD), bf16),
            pltpu.VMEM((STEPS, WIDTH), bf16),
            pltpu.VMEM((STEPS, WIDTH), bf16),
            pltpu.VMEM((WIDTH, 4 * HD), bf16),
            pltpu.VMEM((HD, WIDTH), bf16),
            pltpu.VMEM((STEPS, 4 * HD), f32),
            pltpu.VMEM((STEPS, HD), f32),
            pltpu.VMEM((GROUP, HD), bf16),
            pltpu.VMEM((SLOTS, 2, GROUP, HD), bf16),
            pltpu.VMEM((CAP, 64, HD), jnp.int32),
            pltpu.VMEM((SLOTS * SOURCES, 2 * GROUP), jnp.int32),
            pltpu.VMEM((SLOTS, 2, HD, GROUP), bf16),
            pltpu.VMEM((SLOTS, 2, 8, GROUP), f32),
            pltpu.VMEM((SITES, HD, GROUP), bf16),
            pltpu.VMEM((SITES, 8, GROUP), f32),
            pltpu.VMEM((HD, GROUP), f32),
            pltpu.VMEM((8, GROUP), f32),
            pltpu.VMEM((STEPS, HD), bf16),
            pltpu.VMEM((STEPS, HD), bf16),
            dma((SLOTS,)),
            dma((CHUNKS + 2,)),
            dma,
            dma((3,)),
            dma,
            dma((SLOTS,)),
            dma((SITES,)),
            dma((SLOTS, 2)),
            dma((SLOTS, 2)),
            dma((SITES,)),
            dma((SLOTS, 2)),
            dma((SITES,)),
            dma((2,)),
        ],
        compiler_params=pltpu.CompilerParams(
            collective_id=0, has_side_effects=True, vmem_limit_bytes=56 * 1024 * 1024
        ),
    )(
        new_tokens.reshape(STEPS, WIDTH),
        norm_gain.reshape(1, WIDTH),
        query_weight,
        key_weight.T,
        value_weight.T,
        kv_cache,
        kept_blocks,
        kept_counts,
    )
    attended, entries = pl.pallas_call(
        place,
        out_shape=(
            jax.ShapeDtypeStruct((STEPS, 4 * HD), bf16),
            jax.ShapeDtypeStruct((1, 1, 2 * STEPS * HD), bf16),
        ),
        in_specs=[vmem, vmem],
        out_specs=(vmem, vmem),
    )(attended, entries)
    return attended.reshape(STEPS, 1, 4 * HD), entries


def solution(mesh):
    in_specs = (
        P(None, "seq", None),
        P(),
        P(None, "tp"),
        P(None, "tp"),
        P(None, "tp"),
        P(None, None, ("seq", "tp"), None),
        P(),
        P(),
    )
    out_specs = (P(None, "seq", "tp"), P("seq", "tp", None))
    return jax.shard_map(
        per_device, mesh=mesh, in_specs=in_specs, out_specs=out_specs, check_vma=False
    )
```

```python
import math

import jax
import jax.numpy as jnp
from jax import lax
from jax.experimental import pallas as pl
from jax.experimental.pallas import tpu as pltpu
from jax.sharding import PartitionSpec as P

HD = 128
BLOCK = 64
CAP = 2
STEPS = 64
KEYS = CAP * BLOCK
TOKD = 256
WIDTH = 8192
SLOTS = 4
SOURCES = 16
SITES = 8
GROUP = 256
CHUNKS = 8
CHUNK = WIDTH // CHUNKS
MESH = pl.DeviceIdType.MESH
EXP_SCALE = math.log2(math.e) / math.sqrt(HD)
LOWEST = -1e30

NT = (((1,), (1,)), ((), ()))
TN = (((0,), (0,)), ((), ()))


def kernel(
    tok_hbm,
    gain_hbm,
    wq_hbm,
    wk_hbm,
    wv_hbm,
    kv_hbm,
    kept_hbm,
    counts_hbm,
    att_ref,
    ent_ref,
    gain_ref,
    kept_ref,
    counts_ref,
    kv_buf,
    packed,
    recv,
    tok,
    normed,
    wq,
    wkv,
    q_acc,
    n_acc,
    q_send,
    q_buf,
    pick,
    live_keys,
    o_send,
    l_send,
    o_buf,
    l_buf,
    own_o,
    own_l,
    piece,
    other,
    kv_sem,
    w_sem,
    tok_sem,
    small_sem,
    pack_sem,
    recv_sem,
    q_send_sem,
    q_recv_sem,
    o_send_sem,
    o_recv_sem,
    l_send_sem,
    l_recv_sem,
    piece_sem,
):
    seq = lax.axis_index("seq")
    tp = lax.axis_index("tp")
    z, c = seq // 2, seq % 2
    x, y = tp // 4, tp % 4
    flat = seq * 16 + tp

    def device(x_, y_, z_, c_):
        return (z_ * 2 + c_, x_ * 4 + y_)

    def other_y(y_, odd):
        return (y_ + 1 - 2 * ((y_ + 1 + odd) % 2) + 4) % 4

    def odd_of(x0, z0, c_):
        more = (1 - c_) * (1 - x0 % 2) * (1 - ((z0 - x0 + 4) % 4) // 2)
        return ((x0 + z0) % 2) * (1 - more)

    def pair_at(x_, y_, z_, c_, u, v):
        g = 1 - 2 * c_
        x0, z0 = (x_ - v * g + 4) % 4, (z_ - u * g + 4) % 4
        row = (y_ + odd_of(x0, z0, c_) * (1 + 2 * c_)) % 4
        return x0, z0, row // 2, row % 2

    def kv_start(t):
        u, v = t // 2, t % 2
        for part in range(8):
            dc, dz, dx = part // 4, (part // 2) % 2, part % 2
            c_ = (c + dc) % 2
            g = 1 - 2 * c_
            x0 = (x - dx * g * (2 * v - 1) - v * g + 8) % 4
            z0 = (z - dz * g * (2 * u - 1) - u * g + 8) % 4
            pltpu.make_async_copy(
                kv_hbm.at[:, 2 * z0 + c_, :, pl.ds(pl.multiple_of(x0 * 2 * HD, 2 * HD), 2 * HD)],
                kv_buf.at[t, part],
                kv_sem.at[t],
            ).start()

    def wq_copy(k):
        rows = pl.ds(pl.multiple_of(k * CHUNK, CHUNK), CHUNK)
        return pltpu.make_async_copy(wq_hbm.at[rows], wq.at[rows], w_sem.at[k])

    tok_copy = pltpu.make_async_copy(tok_hbm, tok, tok_sem)
    wk_copy = pltpu.make_async_copy(wk_hbm, wkv.at[pl.ds(0, 64)], w_sem.at[CHUNKS])
    wv_copy = pltpu.make_async_copy(wv_hbm, wkv.at[pl.ds(64, 64)], w_sem.at[CHUNKS + 1])
    gain_copy = pltpu.make_async_copy(gain_hbm, gain_ref, small_sem.at[0])
    kept_copy = pltpu.make_async_copy(kept_hbm, kept_ref, small_sem.at[1])
    counts_copy = pltpu.make_async_copy(counts_hbm, counts_ref, small_sem.at[2])
    kept_copy.start()
    counts_copy.start()
    kv_start(3)
    kv_start(2)
    gain_copy.start()

    barrier = pltpu.get_barrier_semaphore()
    xs = [x, (x + 1) % 4, (x + 3) % 4]
    ys = [y, (y + 1) % 4, (y + 3) % 4, (y + 2) % 4]
    zs = [z, (z + 1) % 4, (z + 3) % 4]
    for i in range(3):
        for j in range(4):
            for k in range(3):
                for c_ in (c, 1 - c)[: 1 if j == 3 else 2]:
                    if i or j or k or c_ is not c:
                        pl.semaphore_signal(
                            barrier,
                            inc=1,
                            device_id=device(xs[i], ys[j], zs[k], c_),
                            device_id_type=MESH,
                        )

    kept_copy.wait()
    counts_copy.wait()
    lane = lax.broadcasted_iota(jnp.int32, (8, 256), 1)
    eye = lax.broadcasted_iota(jnp.int32, (8, 8), 0) == lax.broadcasted_iota(jnp.int32, (8, 8), 1)
    lane_8 = lax.broadcasted_iota(jnp.int32, (1, 8), 1)
    for p in range(8):
        count = jnp.sum(jnp.where(eye, counts_ref[pl.ds(p, 1), :], 0), axis=1, keepdims=True)
        rel = kept_ref[p] - 4 * flat
        code = jnp.where(rel == 0, 1, jnp.where(rel == 1, 2, jnp.where(rel == 2, 4, 8)))
        code = jnp.where((rel >= 0) & (rel < 4) & (lane < count), code, 0)
        mask = jnp.sum(code, axis=1, keepdims=True)
        h0, h1, h2 = mask & 1, (mask >> 1) & 1, (mask >> 2) & 1
        first = jnp.where(h0 == 1, 0, jnp.where(h1 == 1, 1, jnp.where(h2 == 1, 2, 3)))
        second = jnp.where(h0 + h1 == 2, 1, jnp.where((h0 + h1 == 1) & (h2 == 1), 2, 3))
        pick[0, pl.ds(8 * p, 8), :] = jnp.broadcast_to(first, (8, HD))
        pick[1, pl.ds(8 * p, 8), :] = jnp.broadcast_to(second, (8, HD))
    source = lax.broadcasted_iota(jnp.int32, (SOURCES, 256), 0)
    lane_16 = lax.broadcasted_iota(jnp.int32, (SOURCES, 256), 1)
    sx, sy = source >> 3, (source >> 2) & 1
    sz, sc = (source >> 1) & 1, source & 1
    for t in range(SLOTS):
        u, v = t // 2, t % 2
        g = 1 - 2 * c
        x0, z0, hlo, _ = pair_at(x, y, z, c, u, v)
        nx = (x + g * (2 * v - 1) + 4) % 4
        nz = (z + g * (2 * u - 1) + 4) % 4
        ny = other_y(y, odd_of(x0, z0, c))
        fx = jnp.where(sx == 0, x, nx)
        fy = jnp.where(sy == 0, y, ny)
        fz = jnp.where(sz == 0, z, nz)
        fc = jnp.where(sc == 0, c, 1 - c)
        owner = (fz * 2 + fc) * 16 + fx * 4 + fy
        p_, h_ = 2 * z0 + c, 2 * x0 + hlo
        row = kept_ref[p_, pl.ds(h_, 1), :]
        counts = jnp.where(lane_8 == h_, counts_ref[pl.ds(p_, 1), :], 0)
        live = lane_16 < jnp.sum(counts, axis=1, keepdims=True)
        here = jnp.where(live & ((row >> 2) == owner), 1, 0)
        live_keys[pl.ds(16 * t, 16), :] = jnp.broadcast_to(
            BLOCK * jnp.sum(here, axis=1, keepdims=True), (SOURCES, 2 * GROUP)
        )

    def site_of(t, cls):
        u, v = t // 2, t % 2
        dx, dy, dz, c_ = cls // 8, (cls // 4) % 2, (cls // 2) % 2, (c + cls) % 2
        g = 1 - 2 * c_
        x_ = (x - dx * g * (2 * v - 1) + 4) % 4
        z_ = (z - dz * g * (2 * u - 1) + 4) % 4
        odd = odd_of((x_ - v * g + 4) % 4, (z_ - u * g + 4) % 4, c_)
        y_ = y + dy * (other_y(y, odd) - y)
        return x_, y_, z_, c_

    def pack(t, cls, dst):
        x_, y_, z_, c_ = site_of(t, cls)
        x0, z0, hlo, _ = pair_at(x_, y_, z_, c_, t // 2, t % 2)
        part = (cls % 2) * 4 + ((cls // 2) % 2) * 2 + cls // 8
        pair = (2 * z0 + c_) * 8 + 2 * x0 + hlo
        columns = pl.ds(pl.multiple_of(hlo * HD, HD), HD)
        for slot in range(CAP):
            chosen = jnp.broadcast_to(pick[slot, pl.ds(pair, 1), :], (16, HD))
            total = [None, None]
            for block in range(slot, 4):
                weight = jnp.where(chosen == block, 1.0, 0.0).astype(jnp.bfloat16)
                weight = jnp.concatenate([weight] * (BLOCK // 16), axis=0)
                for kind in range(2):
                    rows = kv_buf[t, part, kind, pl.ds(block * BLOCK, BLOCK), columns] * weight
                    total[kind] = rows if total[kind] is None else total[kind] + rows
            for kind in range(2):
                dst[kind, pl.ds(slot * BLOCK, BLOCK), :] = total[kind]

    def pack_slot(t):
        pltpu.make_async_copy(kv_buf.at[t], kv_buf.at[t], kv_sem.at[t]).wait()

        def one(cls, carry):
            pack(t, cls, packed.at[t * 15 + cls - 1])
            return carry

        lax.fori_loop(1, SOURCES, one, 0)

    def send_slot(t):
        def one(i, carry):
            cls = (i * 5) % 16
            pltpu.make_async_remote_copy(
                src_ref=packed.at[t * 15 + cls - 1],
                dst_ref=recv.at[t, cls],
                send_sem=pack_sem,
                recv_sem=recv_sem.at[t],
                device_id=device(*site_of(t, cls)),
                device_id_type=MESH,
            ).start()
            return carry

        lax.fori_loop(1, SOURCES, one, 0)

    pack_slot(3)
    pl.semaphore_wait(barrier, 62)
    send_slot(3)
    tok_copy.start()
    wk_copy.start()
    wv_copy.start()
    for k in range(CHUNKS):
        wq_copy(k).start()
    kv_start(1)
    kv_start(0)
    pack_slot(2)
    send_slot(2)

    tok_copy.wait()
    gain_copy.wait()

    def norm(i, carry):
        rows = pl.ds(pl.multiple_of(i * 16, 16), 16)
        values = tok[rows, :].astype(jnp.float32)
        mean_square = jnp.mean(values * values, axis=-1, keepdims=True)
        normed[rows, :] = (values * lax.rsqrt(mean_square + 1e-05) * gain_ref[...]).astype(
            jnp.bfloat16
        )
        return carry

    lax.fori_loop(0, STEPS // 16, norm, 0)
    wk_copy.wait()
    wv_copy.wait()
    n_acc[...] = jnp.zeros_like(n_acc)
    q_acc[...] = jnp.zeros_like(q_acc)

    def project(k, carry):
        columns = pl.ds(pl.multiple_of(k * CHUNK, CHUNK), CHUNK)
        wq_copy(k).wait()
        rows = normed[:, columns]
        q_acc[...] += jnp.dot(rows, wq[columns, :], preferred_element_type=jnp.float32)
        n_acc[...] += lax.dot_general(rows, wkv[:, columns], NT, preferred_element_type=jnp.float32)
        return carry

    lax.fori_loop(0, CHUNKS, project, 0)

    mine = n_acc[...].astype(jnp.bfloat16)
    piece[...] = mine
    piece_copy = pltpu.make_async_remote_copy(
        src_ref=piece,
        dst_ref=other,
        send_sem=piece_sem.at[0],
        recv_sem=piece_sem.at[1],
        device_id=device(x, y + 1 - 2 * (y % 2), z, c),
        device_id_type=MESH,
    )
    piece_copy.start()
    for g in range(4):
        q_send[pl.ds(g * STEPS, STEPS), :] = q_acc[:, g * HD : (g + 1) * HD].astype(jnp.bfloat16)
    half = y % 2
    toward = 1 - 2 * c
    shift = odd_of(x, z, c) * (1 + 2 * c)

    def site_y(i):
        return (2 * (y // 2) + (i // 2) % 2 - shift + 4) % 4

    def q_copy(i):
        bx, bz = i // 4, i % 2
        return pltpu.make_async_remote_copy(
            src_ref=q_send,
            dst_ref=q_buf.at[2 * bz + bx, half],
            send_sem=q_send_sem.at[i],
            recv_sem=q_recv_sem.at[2 * bz + bx, half],
            device_id=device(
                (x + bx * toward + 4) % 4, site_y(i), (z + bz * toward + 4) % 4, c
            ),
            device_id_type=MESH,
        )

    def is_self(i):
        return (i // 4 == 0) & (i % 2 == 0) & (site_y(i) == y)

    def q_start(i, carry):
        @pl.when(jnp.logical_not(is_self(i)))
        def _():
            q_copy(i).start()

        @pl.when(is_self(i))
        def _():
            q_buf[0, half] = q_send[...]

        return carry

    lax.fori_loop(0, SITES, q_start, 0)

    for t in (1, 0):
        pack_slot(t)
        send_slot(t)

    piece_copy.wait()
    mine = piece[...].astype(jnp.float32)
    theirs = other[...].astype(jnp.float32)
    low = jnp.where(half == 0, mine, theirs)
    high = jnp.where(half == 0, theirs, mine)
    first_half = lax.broadcasted_iota(jnp.int32, (STEPS, HD), 1) < 64
    new_keys = jnp.where(first_half, low, pltpu.roll(high, 64, 1)).astype(jnp.bfloat16)
    new_values = jnp.where(first_half, pltpu.roll(low, 64, 1), high).astype(jnp.bfloat16)
    ent_ref[pl.ds(0, STEPS), :] = new_keys
    ent_ref[pl.ds(STEPS, STEPS), :] = new_values
    scores = lax.dot_general(new_keys, q_send[...], NT, preferred_element_type=jnp.float32)
    key_step = lax.broadcasted_iota(jnp.int32, (STEPS, GROUP), 0)
    row_step = lax.broadcasted_iota(jnp.int32, (STEPS, GROUP), 1) % STEPS
    scores = jnp.where(key_step <= row_step, scores, LOWEST)
    top = jnp.max(scores, axis=0, keepdims=True)
    weights = jnp.exp2((scores - top) * EXP_SCALE)
    own_l[...] = jnp.broadcast_to(
        top * EXP_SCALE + jnp.log2(jnp.sum(weights, axis=0, keepdims=True)), (8, GROUP)
    )
    own_o[...] = lax.dot_general(
        new_values, weights.astype(jnp.bfloat16), TN, preferred_element_type=jnp.float32
    ) / jnp.sum(weights, axis=0, keepdims=True)

    key_row = lax.broadcasted_iota(jnp.int32, (KEYS, 2 * GROUP), 0)

    def home_of(t):
        u, v = t // 2, t % 2
        x0, z0, hlo, by = pair_at(x, y, z, c, u, v)
        near = (t == 0) & (hlo == y // 2)
        return x0, z0, hlo, near, v * 4 + by * 2 + u

    def out_copies(t, m):
        x0, z0, hlo, _, site = home_of(t)
        home = device(x0, 2 * hlo + m, z0, c)
        return (
            pltpu.make_async_remote_copy(
                src_ref=o_send.at[t, m],
                dst_ref=o_buf.at[site],
                send_sem=o_send_sem.at[t, m],
                recv_sem=o_recv_sem.at[site],
                device_id=home,
                device_id_type=MESH,
            ),
            pltpu.make_async_remote_copy(
                src_ref=l_send.at[t, m],
                dst_ref=l_buf.at[site],
                send_sem=l_send_sem.at[t, m],
                recv_sem=l_recv_sem.at[site],
                device_id=home,
                device_id_type=MESH,
            ),
        )

    def attend(step, carry):
        t = SLOTS - 1 - step
        x0, z0, hlo, near, site = home_of(t)
        for m in range(2):

            @pl.when(jnp.logical_not(near & (y % 2 == m)))
            def _(m=m):
                pltpu.make_async_copy(
                    q_buf.at[t, m], q_buf.at[t, m], q_recv_sem.at[t, m]
                ).wait()

        arrived = recv.at[t, pl.ds(1, SOURCES - 1)]
        pltpu.make_async_copy(arrived, arrived, recv_sem.at[t]).wait()
        pack(t, 0, recv.at[t, 0])
        q = q_buf[t].reshape(2 * GROUP, HD)

        keys = recv[t, :, 0].reshape(SOURCES * KEYS, HD)
        values = recv[t, :, 1].reshape(SOURCES * KEYS, HD)
        s = lax.dot_general(keys, q, NT, preferred_element_type=jnp.float32)
        s = jnp.concatenate(
            [
                jnp.where(
                    key_row < live_keys[pl.ds(16 * t + i, 1), :],
                    s[i * KEYS : (i + 1) * KEYS],
                    LOWEST,
                )
                for i in range(SOURCES)
            ],
            axis=0,
        )
        top = jnp.max(s, axis=0, keepdims=True)
        w = jnp.exp2((s - top) * EXP_SCALE)
        total = jnp.sum(w, axis=0, keepdims=True)
        o = lax.dot_general(
            values, w.astype(jnp.bfloat16), TN, preferred_element_type=jnp.float32
        )
        o = (o / total).astype(jnp.bfloat16)
        lse = jnp.broadcast_to(top * EXP_SCALE + jnp.log2(total), (8, 2 * GROUP))
        for m in range(2):
            o_send[t, m] = o[:, m * GROUP : (m + 1) * GROUP]
            l_send[t, m] = lse[:, m * GROUP : (m + 1) * GROUP]
            leaves = jnp.logical_not(near & (y % 2 == m))

            @pl.when(leaves)
            def _(m=m):
                for copy in out_copies(t, m):
                    copy.start()

            @pl.when(jnp.logical_not(leaves))
            def _(m=m):
                o_buf[site] = o_send[t, m]
                l_buf[site] = l_send[t, m]

        return carry

    lax.fori_loop(0, SLOTS, attend, 0)

    def await_site(i, carry):
        @pl.when(jnp.logical_not(is_self(i)))
        def _():
            pltpu.make_async_copy(o_buf.at[i], o_buf.at[i], o_recv_sem.at[i]).wait()
            pltpu.make_async_copy(l_buf.at[i], l_buf.at[i], l_recv_sem.at[i]).wait()

        return carry

    lax.fori_loop(0, SITES, await_site, 0)
    top = own_l[pl.ds(0, 1), :]
    for i in range(SITES):
        top = jnp.maximum(top, l_buf[i, pl.ds(0, 1), :])
    share = jnp.exp2(own_l[pl.ds(0, 1), :] - top)
    total = share
    result = own_o[...] * share
    for i in range(SITES):
        share = jnp.exp2(l_buf[i, pl.ds(0, 1), :] - top)
        total = total + share
        result = result + o_buf[i].astype(jnp.float32) * share
    result = (result / total).T
    for g in range(4):
        att_ref[:, g * HD : (g + 1) * HD] = result[g * STEPS : (g + 1) * STEPS, :].astype(
            jnp.bfloat16
        )

    pltpu.make_async_copy(packed, packed, pack_sem).wait()

    def await_q(i, carry):
        @pl.when(jnp.logical_not(is_self(i)))
        def _():
            q_copy(i).wait_send()

        return carry

    lax.fori_loop(0, SITES, await_q, 0)

    def await_out(t, carry):
        _, _, _, near, _ = home_of(t)
        for m in range(2):

            @pl.when(jnp.logical_not(near & (y % 2 == m)))
            def _(m=m):
                for copy in out_copies(t, m):
                    copy.wait_send()

        return carry

    lax.fori_loop(0, SLOTS, await_out, 0)


def place(att_ref, ent_ref, att_out, ent_out):
    att_out[...] = att_ref[...]
    for row in range(2 * STEPS):
        ent_out[0, :, row * HD : (row + 1) * HD] = ent_ref[row : row + 1, :]


def per_device(
    new_tokens,
    norm_gain,
    query_weight,
    key_weight,
    value_weight,
    kv_cache,
    kept_blocks,
    kept_counts,
):
    vmem = pl.BlockSpec(memory_space=pltpu.VMEM)
    hbm = pl.BlockSpec(memory_space=pl.ANY)
    bf16, f32 = jnp.bfloat16, jnp.float32
    dma = pltpu.SemaphoreType.DMA
    attended, entries = pl.pallas_call(
        kernel,
        out_shape=(
            jax.ShapeDtypeStruct((STEPS, 4 * HD), bf16),
            jax.ShapeDtypeStruct((2 * STEPS, HD), bf16),
        ),
        in_specs=[hbm] * 8,
        out_specs=(vmem, vmem),
        scratch_shapes=[
            pltpu.VMEM((1, WIDTH), f32),
            pltpu.VMEM((8, 8, 256), jnp.int32),
            pltpu.VMEM((8, 8), jnp.int32),
            pltpu.VMEM((SLOTS, 8, 2, TOKD, 2 * HD), bf16),
            pltpu.VMEM((SLOTS * (SOURCES - 1), 2, KEYS, HD), bf16),
            pltpu.VMEM((SLOTS, SOURCES, 2, KEYS, HD), bf16),
            pltpu.VMEM((STEPS, WIDTH), bf16),
            pltpu.VMEM((STEPS, WIDTH), bf16),
            pltpu.VMEM((WIDTH, 4 * HD), bf16),
            pltpu.VMEM((HD, WIDTH), bf16),
            pltpu.VMEM((STEPS, 4 * HD), f32),
            pltpu.VMEM((STEPS, HD), f32),
            pltpu.VMEM((GROUP, HD), bf16),
            pltpu.VMEM((SLOTS, 2, GROUP, HD), bf16),
            pltpu.VMEM((CAP, 64, HD), jnp.int32),
            pltpu.VMEM((SLOTS * SOURCES, 2 * GROUP), jnp.int32),
            pltpu.VMEM((SLOTS, 2, HD, GROUP), bf16),
            pltpu.VMEM((SLOTS, 2, 8, GROUP), f32),
            pltpu.VMEM((SITES, HD, GROUP), bf16),
            pltpu.VMEM((SITES, 8, GROUP), f32),
            pltpu.VMEM((HD, GROUP), f32),
            pltpu.VMEM((8, GROUP), f32),
            pltpu.VMEM((STEPS, HD), bf16),
            pltpu.VMEM((STEPS, HD), bf16),
            dma((SLOTS,)),
            dma((CHUNKS + 2,)),
            dma,
            dma((3,)),
            dma,
            dma((SLOTS,)),
            dma((SITES,)),
            dma((SLOTS, 2)),
            dma((SLOTS, 2)),
            dma((SITES,)),
            dma((SLOTS, 2)),
            dma((SITES,)),
            dma((2,)),
        ],
        compiler_params=pltpu.CompilerParams(
            collective_id=0, has_side_effects=True, vmem_limit_bytes=56 * 1024 * 1024
        ),
    )(
        new_tokens.reshape(STEPS, WIDTH),
        norm_gain.reshape(1, WIDTH),
        query_weight,
        key_weight.T,
        value_weight.T,
        kv_cache,
        kept_blocks,
        kept_counts,
    )
    attended, entries = pl.pallas_call(
        place,
        out_shape=(
            jax.ShapeDtypeStruct((STEPS, 4 * HD), bf16),
            jax.ShapeDtypeStruct((1, 1, 2 * STEPS * HD), bf16),
        ),
        in_specs=[vmem, vmem],
        out_specs=(vmem, vmem),
    )(attended, entries)
    return attended.reshape(STEPS, 1, 4 * HD), entries


def solution(mesh):
    in_specs = (
        P(None, "seq", None),
        P(),
        P(None, "tp"),
        P(None, "tp"),
        P(None, "tp"),
        P(None, None, ("seq", "tp"), None),
        P(),
        P(),
    )
    out_specs = (P(None, "seq", "tp"), P("seq", "tp", None))
    return jax.shard_map(
        per_device, mesh=mesh, in_specs=in_specs, out_specs=out_specs, check_vma=False
    )
```

```python
import math

import jax
import jax.numpy as jnp
from jax import lax
from jax.experimental import pallas as pl
from jax.experimental.pallas import tpu as pltpu
from jax.sharding import PartitionSpec as P

HD = 128
BLOCK = 64
CAP = 2
STEPS = 64
KEYS = CAP * BLOCK
TOKD = 256
WIDTH = 8192
SLOTS = 4
SOURCES = 16
SITES = 8
GROUP = 256
CHUNKS = 8
CHUNK = WIDTH // CHUNKS
MESH = pl.DeviceIdType.MESH
EXP_SCALE = math.log2(math.e) / math.sqrt(HD)
LOWEST = -1e30

NT = (((1,), (1,)), ((), ()))
TN = (((0,), (0,)), ((), ()))


def kernel(
    tok_hbm,
    gain_hbm,
    wq_hbm,
    wk_hbm,
    wv_hbm,
    kv_hbm,
    kept_hbm,
    counts_hbm,
    att_ref,
    ent_ref,
    gain_ref,
    kept_ref,
    counts_ref,
    kv_buf,
    packed,
    recv,
    tok,
    normed,
    wq,
    wkv,
    q_acc,
    n_acc,
    q_send,
    q_buf,
    pick,
    live_keys,
    o_send,
    l_send,
    o_buf,
    l_buf,
    own_o,
    own_l,
    piece,
    other,
    kv_sem,
    w_sem,
    tok_sem,
    small_sem,
    pack_sem,
    recv_sem,
    q_send_sem,
    q_recv_sem,
    o_send_sem,
    o_recv_sem,
    l_send_sem,
    l_recv_sem,
    piece_sem,
):
    seq = lax.axis_index("seq")
    tp = lax.axis_index("tp")
    z, c = seq // 2, seq % 2
    x, y = tp // 4, tp % 4
    flat = seq * 16 + tp

    def device(x_, y_, z_, c_):
        return (z_ * 2 + c_, x_ * 4 + y_)

    def other_y(y_, odd):
        return (y_ + 1 - 2 * ((y_ + 1 + odd) % 2) + 4) % 4

    def odd_of(x0, z0, c_):
        more = (1 - c_) * (1 - x0 % 2) * (1 - ((z0 - x0 + 4) % 4) // 2)
        return ((x0 + z0) % 2) * (1 - more)

    def pair_at(x_, y_, z_, c_, u, v):
        g = 1 - 2 * c_
        x0, z0 = (x_ - v * g + 4) % 4, (z_ - u * g + 4) % 4
        row = (y_ + odd_of(x0, z0, c_) * (1 + 2 * c_)) % 4
        return x0, z0, row // 2, row % 2

    def kv_start(t):
        u, v = t // 2, t % 2
        for part in range(8):
            dc, dz, dx = part // 4, (part // 2) % 2, part % 2
            c_ = (c + dc) % 2
            g = 1 - 2 * c_
            x0 = (x - dx * g * (2 * v - 1) - v * g + 8) % 4
            z0 = (z - dz * g * (2 * u - 1) - u * g + 8) % 4
            pltpu.make_async_copy(
                kv_hbm.at[:, 2 * z0 + c_, :, pl.ds(pl.multiple_of(x0 * 2 * HD, 2 * HD), 2 * HD)],
                kv_buf.at[t, part],
                kv_sem.at[t],
            ).start()

    def wq_copy(k):
        rows = pl.ds(pl.multiple_of(k * CHUNK, CHUNK), CHUNK)
        return pltpu.make_async_copy(wq_hbm.at[rows], wq.at[rows], w_sem.at[k])

    tok_copy = pltpu.make_async_copy(tok_hbm, tok, tok_sem)
    wk_copy = pltpu.make_async_copy(wk_hbm, wkv.at[pl.ds(0, 64)], w_sem.at[CHUNKS])
    wv_copy = pltpu.make_async_copy(wv_hbm, wkv.at[pl.ds(64, 64)], w_sem.at[CHUNKS + 1])
    gain_copy = pltpu.make_async_copy(gain_hbm, gain_ref, small_sem.at[0])
    kept_copy = pltpu.make_async_copy(kept_hbm, kept_ref, small_sem.at[1])
    counts_copy = pltpu.make_async_copy(counts_hbm, counts_ref, small_sem.at[2])
    kept_copy.start()
    counts_copy.start()
    kv_start(3)
    kv_start(2)
    gain_copy.start()

    barrier = pltpu.get_barrier_semaphore()
    xs = [x, (x + 1) % 4, (x + 3) % 4]
    ys = [y, (y + 1) % 4, (y + 3) % 4, (y + 2) % 4]
    zs = [z, (z + 1) % 4, (z + 3) % 4]
    for i in range(3):
        for j in range(4):
            for k in range(3):
                for c_ in (c, 1 - c)[: 1 if j == 3 else 2]:
                    if i or j or k or c_ is not c:
                        pl.semaphore_signal(
                            barrier,
                            inc=1,
                            device_id=device(xs[i], ys[j], zs[k], c_),
                            device_id_type=MESH,
                        )

    kept_copy.wait()
    counts_copy.wait()
    lane = lax.broadcasted_iota(jnp.int32, (8, 256), 1)
    eye = lax.broadcasted_iota(jnp.int32, (8, 8), 0) == lax.broadcasted_iota(jnp.int32, (8, 8), 1)
    lane_8 = lax.broadcasted_iota(jnp.int32, (1, 8), 1)
    for p in range(8):
        count = jnp.sum(jnp.where(eye, counts_ref[pl.ds(p, 1), :], 0), axis=1, keepdims=True)
        rel = kept_ref[p] - 4 * flat
        code = jnp.where(rel == 0, 1, jnp.where(rel == 1, 2, jnp.where(rel == 2, 4, 8)))
        code = jnp.where((rel >= 0) & (rel < 4) & (lane < count), code, 0)
        mask = jnp.sum(code, axis=1, keepdims=True)
        h0, h1, h2 = mask & 1, (mask >> 1) & 1, (mask >> 2) & 1
        first = jnp.where(h0 == 1, 0, jnp.where(h1 == 1, 1, jnp.where(h2 == 1, 2, 3)))
        second = jnp.where(h0 + h1 == 2, 1, jnp.where((h0 + h1 == 1) & (h2 == 1), 2, 3))
        pick[0, pl.ds(8 * p, 8), :] = jnp.broadcast_to(first, (8, HD))
        pick[1, pl.ds(8 * p, 8), :] = jnp.broadcast_to(second, (8, HD))
    source = lax.broadcasted_iota(jnp.int32, (SOURCES, 256), 0)
    lane_16 = lax.broadcasted_iota(jnp.int32, (SOURCES, 256), 1)
    sx, sy = source >> 3, (source >> 2) & 1
    sz, sc = (source >> 1) & 1, source & 1
    for t in range(SLOTS):
        u, v = t // 2, t % 2
        g = 1 - 2 * c
        x0, z0, hlo, _ = pair_at(x, y, z, c, u, v)
        nx = (x + g * (2 * v - 1) + 4) % 4
        nz = (z + g * (2 * u - 1) + 4) % 4
        ny = other_y(y, odd_of(x0, z0, c))
        fx = jnp.where(sx == 0, x, nx)
        fy = jnp.where(sy == 0, y, ny)
        fz = jnp.where(sz == 0, z, nz)
        fc = jnp.where(sc == 0, c, 1 - c)
        owner = (fz * 2 + fc) * 16 + fx * 4 + fy
        p_, h_ = 2 * z0 + c, 2 * x0 + hlo
        row = kept_ref[p_, pl.ds(h_, 1), :]
        counts = jnp.where(lane_8 == h_, counts_ref[pl.ds(p_, 1), :], 0)
        live = lane_16 < jnp.sum(counts, axis=1, keepdims=True)
        here = jnp.where(live & ((row >> 2) == owner), 1, 0)
        live_keys[pl.ds(16 * t, 16), :] = jnp.broadcast_to(
            BLOCK * jnp.sum(here, axis=1, keepdims=True), (SOURCES, 2 * GROUP)
        )

    def site_of(t, cls):
        u, v = t // 2, t % 2
        dx, dy, dz, c_ = cls // 8, (cls // 4) % 2, (cls // 2) % 2, (c + cls) % 2
        g = 1 - 2 * c_
        x_ = (x - dx * g * (2 * v - 1) + 4) % 4
        z_ = (z - dz * g * (2 * u - 1) + 4) % 4
        odd = odd_of((x_ - v * g + 4) % 4, (z_ - u * g + 4) % 4, c_)
        y_ = y + dy * (other_y(y, odd) - y)
        return x_, y_, z_, c_

    def pack(t, cls, dst):
        x_, y_, z_, c_ = site_of(t, cls)
        x0, z0, hlo, _ = pair_at(x_, y_, z_, c_, t // 2, t % 2)
        part = (cls % 2) * 4 + ((cls // 2) % 2) * 2 + cls // 8
        pair = (2 * z0 + c_) * 8 + 2 * x0 + hlo
        columns = pl.ds(pl.multiple_of(hlo * HD, HD), HD)
        for slot in range(CAP):
            chosen = jnp.broadcast_to(pick[slot, pl.ds(pair, 1), :], (16, HD))
            total = [None, None]
            for block in range(slot, 4):
                weight = jnp.where(chosen == block, 1.0, 0.0).astype(jnp.bfloat16)
                weight = jnp.concatenate([weight] * (BLOCK // 16), axis=0)
                for kind in range(2):
                    rows = kv_buf[t, part, kind, pl.ds(block * BLOCK, BLOCK), columns] * weight
                    total[kind] = rows if total[kind] is None else total[kind] + rows
            for kind in range(2):
                dst[kind, pl.ds(slot * BLOCK, BLOCK), :] = total[kind]

    def pack_slot(t):
        pltpu.make_async_copy(kv_buf.at[t], kv_buf.at[t], kv_sem.at[t]).wait()

        def one(cls, carry):
            pack(t, cls, packed.at[t * 15 + cls - 1])
            return carry

        lax.fori_loop(1, SOURCES, one, 0)

    def send_slot(t):
        def one(i, carry):
            cls = (i * (5 + 2 * c)) % 16
            pltpu.make_async_remote_copy(
                src_ref=packed.at[t * 15 + cls - 1],
                dst_ref=recv.at[t, cls],
                send_sem=pack_sem,
                recv_sem=recv_sem.at[t],
                device_id=device(*site_of(t, cls)),
                device_id_type=MESH,
            ).start()
            return carry

        lax.fori_loop(1, SOURCES, one, 0)

    pack_slot(3)
    pl.semaphore_wait(barrier, 62)
    send_slot(3)
    tok_copy.start()
    wk_copy.start()
    wv_copy.start()
    for k in range(CHUNKS):
        wq_copy(k).start()
    kv_start(1)
    kv_start(0)
    pack_slot(2)
    send_slot(2)

    tok_copy.wait()
    gain_copy.wait()

    def norm(i, carry):
        rows = pl.ds(pl.multiple_of(i * 16, 16), 16)
        values = tok[rows, :].astype(jnp.float32)
        mean_square = jnp.mean(values * values, axis=-1, keepdims=True)
        normed[rows, :] = (values * lax.rsqrt(mean_square + 1e-05) * gain_ref[...]).astype(
            jnp.bfloat16
        )
        return carry

    lax.fori_loop(0, STEPS // 16, norm, 0)
    wk_copy.wait()
    wv_copy.wait()
    n_acc[...] = jnp.zeros_like(n_acc)
    q_acc[...] = jnp.zeros_like(q_acc)

    def project(k, carry):
        columns = pl.ds(pl.multiple_of(k * CHUNK, CHUNK), CHUNK)
        wq_copy(k).wait()
        rows = normed[:, columns]
        q_acc[...] += jnp.dot(rows, wq[columns, :], preferred_element_type=jnp.float32)
        n_acc[...] += lax.dot_general(rows, wkv[:, columns], NT, preferred_element_type=jnp.float32)
        return carry

    lax.fori_loop(0, CHUNKS, project, 0)

    mine = n_acc[...].astype(jnp.bfloat16)
    piece[...] = mine
    piece_copy = pltpu.make_async_remote_copy(
        src_ref=piece,
        dst_ref=other,
        send_sem=piece_sem.at[0],
        recv_sem=piece_sem.at[1],
        device_id=device(x, y + 1 - 2 * (y % 2), z, c),
        device_id_type=MESH,
    )
    piece_copy.start()
    for g in range(4):
        q_send[pl.ds(g * STEPS, STEPS), :] = q_acc[:, g * HD : (g + 1) * HD].astype(jnp.bfloat16)
    half = y % 2
    toward = 1 - 2 * c
    shift = odd_of(x, z, c) * (1 + 2 * c)

    def site_y(i):
        return (2 * (y // 2) + (i // 2) % 2 - shift + 4) % 4

    def q_copy(i):
        bx, bz = i // 4, i % 2
        return pltpu.make_async_remote_copy(
            src_ref=q_send,
            dst_ref=q_buf.at[2 * bz + bx, half],
            send_sem=q_send_sem.at[i],
            recv_sem=q_recv_sem.at[2 * bz + bx, half],
            device_id=device(
                (x + bx * toward + 4) % 4, site_y(i), (z + bz * toward + 4) % 4, c
            ),
            device_id_type=MESH,
        )

    def is_self(i):
        return (i // 4 == 0) & (i % 2 == 0) & (site_y(i) == y)

    def q_start(i, carry):
        @pl.when(jnp.logical_not(is_self(i)))
        def _():
            q_copy(i).start()

        @pl.when(is_self(i))
        def _():
            q_buf[0, half] = q_send[...]

        return carry

    lax.fori_loop(0, SITES, q_start, 0)

    for t in (1, 0):
        pack_slot(t)
        send_slot(t)

    piece_copy.wait()
    mine = piece[...].astype(jnp.float32)
    theirs = other[...].astype(jnp.float32)
    low = jnp.where(half == 0, mine, theirs)
    high = jnp.where(half == 0, theirs, mine)
    first_half = lax.broadcasted_iota(jnp.int32, (STEPS, HD), 1) < 64
    new_keys = jnp.where(first_half, low, pltpu.roll(high, 64, 1)).astype(jnp.bfloat16)
    new_values = jnp.where(first_half, pltpu.roll(low, 64, 1), high).astype(jnp.bfloat16)
    ent_ref[pl.ds(0, STEPS), :] = new_keys
    ent_ref[pl.ds(STEPS, STEPS), :] = new_values
    scores = lax.dot_general(new_keys, q_send[...], NT, preferred_element_type=jnp.float32)
    key_step = lax.broadcasted_iota(jnp.int32, (STEPS, GROUP), 0)
    row_step = lax.broadcasted_iota(jnp.int32, (STEPS, GROUP), 1) % STEPS
    scores = jnp.where(key_step <= row_step, scores, LOWEST)
    top = jnp.max(scores, axis=0, keepdims=True)
    weights = jnp.exp2((scores - top) * EXP_SCALE)
    own_l[...] = jnp.broadcast_to(
        top * EXP_SCALE + jnp.log2(jnp.sum(weights, axis=0, keepdims=True)), (8, GROUP)
    )
    own_o[...] = lax.dot_general(
        new_values, weights.astype(jnp.bfloat16), TN, preferred_element_type=jnp.float32
    ) / jnp.sum(weights, axis=0, keepdims=True)

    key_row = lax.broadcasted_iota(jnp.int32, (KEYS, 2 * GROUP), 0)

    def home_of(t):
        u, v = t // 2, t % 2
        x0, z0, hlo, by = pair_at(x, y, z, c, u, v)
        near = (t == 0) & (hlo == y // 2)
        return x0, z0, hlo, near, v * 4 + by * 2 + u

    def out_copies(t, m):
        x0, z0, hlo, _, site = home_of(t)
        home = device(x0, 2 * hlo + m, z0, c)
        return (
            pltpu.make_async_remote_copy(
                src_ref=o_send.at[t, m],
                dst_ref=o_buf.at[site],
                send_sem=o_send_sem.at[t, m],
                recv_sem=o_recv_sem.at[site],
                device_id=home,
                device_id_type=MESH,
            ),
            pltpu.make_async_remote_copy(
                src_ref=l_send.at[t, m],
                dst_ref=l_buf.at[site],
                send_sem=l_send_sem.at[t, m],
                recv_sem=l_recv_sem.at[site],
                device_id=home,
                device_id_type=MESH,
            ),
        )

    def attend(step, carry):
        t = SLOTS - 1 - step
        x0, z0, hlo, near, site = home_of(t)
        for m in range(2):

            @pl.when(jnp.logical_not(near & (y % 2 == m)))
            def _(m=m):
                pltpu.make_async_copy(
                    q_buf.at[t, m], q_buf.at[t, m], q_recv_sem.at[t, m]
                ).wait()

        arrived = recv.at[t, pl.ds(1, SOURCES - 1)]
        pltpu.make_async_copy(arrived, arrived, recv_sem.at[t]).wait()
        pack(t, 0, recv.at[t, 0])
        q = q_buf[t].reshape(2 * GROUP, HD)

        keys = recv[t, :, 0].reshape(SOURCES * KEYS, HD)
        values = recv[t, :, 1].reshape(SOURCES * KEYS, HD)
        s = lax.dot_general(keys, q, NT, preferred_element_type=jnp.float32)
        s = jnp.concatenate(
            [
                jnp.where(
                    key_row < live_keys[pl.ds(16 * t + i, 1), :],
                    s[i * KEYS : (i + 1) * KEYS],
                    LOWEST,
                )
                for i in range(SOURCES)
            ],
            axis=0,
        )
        top = jnp.max(s, axis=0, keepdims=True)
        w = jnp.exp2((s - top) * EXP_SCALE)
        total = jnp.sum(w, axis=0, keepdims=True)
        o = lax.dot_general(
            values, w.astype(jnp.bfloat16), TN, preferred_element_type=jnp.float32
        )
        o = (o / total).astype(jnp.bfloat16)
        lse = jnp.broadcast_to(top * EXP_SCALE + jnp.log2(total), (8, 2 * GROUP))
        for m in range(2):
            o_send[t, m] = o[:, m * GROUP : (m + 1) * GROUP]
            l_send[t, m] = lse[:, m * GROUP : (m + 1) * GROUP]
            leaves = jnp.logical_not(near & (y % 2 == m))

            @pl.when(leaves)
            def _(m=m):
                for copy in out_copies(t, m):
                    copy.start()

            @pl.when(jnp.logical_not(leaves))
            def _(m=m):
                o_buf[site] = o_send[t, m]
                l_buf[site] = l_send[t, m]

        return carry

    lax.fori_loop(0, SLOTS, attend, 0)

    def await_site(i, carry):
        @pl.when(jnp.logical_not(is_self(i)))
        def _():
            pltpu.make_async_copy(o_buf.at[i], o_buf.at[i], o_recv_sem.at[i]).wait()
            pltpu.make_async_copy(l_buf.at[i], l_buf.at[i], l_recv_sem.at[i]).wait()

        return carry

    lax.fori_loop(0, SITES, await_site, 0)
    top = own_l[pl.ds(0, 1), :]
    for i in range(SITES):
        top = jnp.maximum(top, l_buf[i, pl.ds(0, 1), :])
    share = jnp.exp2(own_l[pl.ds(0, 1), :] - top)
    total = share
    result = own_o[...] * share
    for i in range(SITES):
        share = jnp.exp2(l_buf[i, pl.ds(0, 1), :] - top)
        total = total + share
        result = result + o_buf[i].astype(jnp.float32) * share
    result = (result / total).T
    for g in range(4):
        att_ref[:, g * HD : (g + 1) * HD] = result[g * STEPS : (g + 1) * STEPS, :].astype(
            jnp.bfloat16
        )

    pltpu.make_async_copy(packed, packed, pack_sem).wait()

    def await_q(i, carry):
        @pl.when(jnp.logical_not(is_self(i)))
        def _():
            q_copy(i).wait_send()

        return carry

    lax.fori_loop(0, SITES, await_q, 0)

    def await_out(t, carry):
        _, _, _, near, _ = home_of(t)
        for m in range(2):

            @pl.when(jnp.logical_not(near & (y % 2 == m)))
            def _(m=m):
                for copy in out_copies(t, m):
                    copy.wait_send()

        return carry

    lax.fori_loop(0, SLOTS, await_out, 0)


def place(att_ref, ent_ref, att_out, ent_out):
    att_out[...] = att_ref[...]
    for row in range(2 * STEPS):
        ent_out[0, :, row * HD : (row + 1) * HD] = ent_ref[row : row + 1, :]


def per_device(
    new_tokens,
    norm_gain,
    query_weight,
    key_weight,
    value_weight,
    kv_cache,
    kept_blocks,
    kept_counts,
):
    vmem = pl.BlockSpec(memory_space=pltpu.VMEM)
    hbm = pl.BlockSpec(memory_space=pl.ANY)
    bf16, f32 = jnp.bfloat16, jnp.float32
    dma = pltpu.SemaphoreType.DMA
    attended, entries = pl.pallas_call(
        kernel,
        out_shape=(
            jax.ShapeDtypeStruct((STEPS, 4 * HD), bf16),
            jax.ShapeDtypeStruct((2 * STEPS, HD), bf16),
        ),
        in_specs=[hbm] * 8,
        out_specs=(vmem, vmem),
        scratch_shapes=[
            pltpu.VMEM((1, WIDTH), f32),
            pltpu.VMEM((8, 8, 256), jnp.int32),
            pltpu.VMEM((8, 8), jnp.int32),
            pltpu.VMEM((SLOTS, 8, 2, TOKD, 2 * HD), bf16),
            pltpu.VMEM((SLOTS * (SOURCES - 1), 2, KEYS, HD), bf16),
            pltpu.VMEM((SLOTS, SOURCES, 2, KEYS, HD), bf16),
            pltpu.VMEM((STEPS, WIDTH), bf16),
            pltpu.VMEM((STEPS, WIDTH), bf16),
            pltpu.VMEM((WIDTH, 4 * HD), bf16),
            pltpu.VMEM((HD, WIDTH), bf16),
            pltpu.VMEM((STEPS, 4 * HD), f32),
            pltpu.VMEM((STEPS, HD), f32),
            pltpu.VMEM((GROUP, HD), bf16),
            pltpu.VMEM((SLOTS, 2, GROUP, HD), bf16),
            pltpu.VMEM((CAP, 64, HD), jnp.int32),
            pltpu.VMEM((SLOTS * SOURCES, 2 * GROUP), jnp.int32),
            pltpu.VMEM((SLOTS, 2, HD, GROUP), bf16),
            pltpu.VMEM((SLOTS, 2, 8, GROUP), f32),
            pltpu.VMEM((SITES, HD, GROUP), bf16),
            pltpu.VMEM((SITES, 8, GROUP), f32),
            pltpu.VMEM((HD, GROUP), f32),
            pltpu.VMEM((8, GROUP), f32),
            pltpu.VMEM((STEPS, HD), bf16),
            pltpu.VMEM((STEPS, HD), bf16),
            dma((SLOTS,)),
            dma((CHUNKS + 2,)),
            dma,
            dma((3,)),
            dma,
            dma((SLOTS,)),
            dma((SITES,)),
            dma((SLOTS, 2)),
            dma((SLOTS, 2)),
            dma((SITES,)),
            dma((SLOTS, 2)),
            dma((SITES,)),
            dma((2,)),
        ],
        compiler_params=pltpu.CompilerParams(
            collective_id=0, has_side_effects=True, vmem_limit_bytes=56 * 1024 * 1024
        ),
    )(
        new_tokens.reshape(STEPS, WIDTH),
        norm_gain.reshape(1, WIDTH),
        query_weight,
        key_weight.T,
        value_weight.T,
        kv_cache,
        kept_blocks,
        kept_counts,
    )
    attended, entries = pl.pallas_call(
        place,
        out_shape=(
            jax.ShapeDtypeStruct((STEPS, 4 * HD), bf16),
            jax.ShapeDtypeStruct((1, 1, 2 * STEPS * HD), bf16),
        ),
        in_specs=[vmem, vmem],
        out_specs=(vmem, vmem),
    )(attended, entries)
    return attended.reshape(STEPS, 1, 4 * HD), entries


def solution(mesh):
    in_specs = (
        P(None, "seq", None),
        P(),
        P(None, "tp"),
        P(None, "tp"),
        P(None, "tp"),
        P(None, None, ("seq", "tp"), None),
        P(),
        P(),
    )
    out_specs = (P(None, "seq", "tp"), P("seq", "tp", None))
    return jax.shard_map(
        per_device, mesh=mesh, in_specs=in_specs, out_specs=out_specs, check_vma=False
    )
```

```python
import math

import jax
import jax.numpy as jnp
from jax import lax
from jax.experimental import pallas as pl
from jax.experimental.pallas import tpu as pltpu
from jax.sharding import PartitionSpec as P

HD = 128
BLOCK = 64
CAP = 2
STEPS = 64
KEYS = CAP * BLOCK
TOKD = 256
WIDTH = 8192
SLOTS = 4
SOURCES = 16
SITES = 8
GROUP = 256
CHUNKS = 8
CHUNK = WIDTH // CHUNKS
MESH = pl.DeviceIdType.MESH
EXP_SCALE = math.log2(math.e) / math.sqrt(HD)
LOWEST = -1e30

NT = (((1,), (1,)), ((), ()))
TN = (((0,), (0,)), ((), ()))


def kernel(
    tok_hbm,
    gain_hbm,
    wq_hbm,
    wk_hbm,
    wv_hbm,
    kv_hbm,
    kept_hbm,
    counts_hbm,
    att_ref,
    ent_ref,
    gain_ref,
    kept_ref,
    counts_ref,
    kv_buf,
    packed,
    recv,
    tok,
    normed,
    wq,
    wkv,
    q_acc,
    n_acc,
    q_send,
    q_buf,
    pick,
    live_keys,
    o_send,
    l_send,
    o_buf,
    l_buf,
    own_o,
    own_l,
    piece,
    other,
    kv_sem,
    w_sem,
    tok_sem,
    small_sem,
    pack_sem,
    recv_sem,
    q_send_sem,
    q_recv_sem,
    o_send_sem,
    o_recv_sem,
    l_send_sem,
    l_recv_sem,
    piece_sem,
):
    seq = lax.axis_index("seq")
    tp = lax.axis_index("tp")
    z, c = seq // 2, seq % 2
    x, y = tp // 4, tp % 4
    flat = seq * 16 + tp

    def device(x_, y_, z_, c_):
        return (z_ * 2 + c_, x_ * 4 + y_)

    def other_y(y_, odd):
        return (y_ + 1 - 2 * ((y_ + 1 + odd) % 2) + 4) % 4

    def odd_of(x0, z0, c_):
        more = (1 - c_) * (1 - x0 % 2) * (1 - ((z0 - x0 + 4) % 4) // 2)
        return ((x0 + z0) % 2) * (1 - more)

    def pair_at(x_, y_, z_, c_, u, v):
        g = 1 - 2 * c_
        x0, z0 = (x_ - v * g + 4) % 4, (z_ - u * g + 4) % 4
        row = (y_ + odd_of(x0, z0, c_) * (1 + 2 * c_)) % 4
        return x0, z0, row // 2, row % 2

    def kv_start(t):
        u, v = t // 2, t % 2
        for part in range(8):
            dc, dz, dx = part // 4, (part // 2) % 2, part % 2
            c_ = (c + dc) % 2
            g = 1 - 2 * c_
            x0 = (x - dx * g * (2 * v - 1) - v * g + 8) % 4
            z0 = (z - dz * g * (2 * u - 1) - u * g + 8) % 4
            pltpu.make_async_copy(
                kv_hbm.at[:, 2 * z0 + c_, :, pl.ds(pl.multiple_of(x0 * 2 * HD, 2 * HD), 2 * HD)],
                kv_buf.at[t, part],
                kv_sem.at[t],
            ).start()

    def wq_copy(k):
        rows = pl.ds(pl.multiple_of(k * CHUNK, CHUNK), CHUNK)
        return pltpu.make_async_copy(wq_hbm.at[rows], wq.at[rows], w_sem.at[k])

    tok_copy = pltpu.make_async_copy(tok_hbm, tok, tok_sem)
    wk_copy = pltpu.make_async_copy(wk_hbm, wkv.at[pl.ds(0, 64)], w_sem.at[CHUNKS])
    wv_copy = pltpu.make_async_copy(wv_hbm, wkv.at[pl.ds(64, 64)], w_sem.at[CHUNKS + 1])
    gain_copy = pltpu.make_async_copy(gain_hbm, gain_ref, small_sem.at[0])
    kept_copy = pltpu.make_async_copy(kept_hbm, kept_ref, small_sem.at[1])
    counts_copy = pltpu.make_async_copy(counts_hbm, counts_ref, small_sem.at[2])
    kept_copy.start()
    counts_copy.start()
    kv_start(3)
    kv_start(2)
    gain_copy.start()

    barrier = pltpu.get_barrier_semaphore()
    xs = [x, (x + 1) % 4, (x + 3) % 4]
    ys = [y, (y + 1) % 4, (y + 3) % 4, (y + 2) % 4]
    zs = [z, (z + 1) % 4, (z + 3) % 4]
    for i in range(3):
        for j in range(4):
            for k in range(3):
                for c_ in (c, 1 - c)[: 1 if j == 3 else 2]:
                    if i or j or k or c_ is not c:
                        pl.semaphore_signal(
                            barrier,
                            inc=1,
                            device_id=device(xs[i], ys[j], zs[k], c_),
                            device_id_type=MESH,
                        )

    kept_copy.wait()
    counts_copy.wait()
    lane = lax.broadcasted_iota(jnp.int32, (8, 256), 1)
    eye = lax.broadcasted_iota(jnp.int32, (8, 8), 0) == lax.broadcasted_iota(jnp.int32, (8, 8), 1)
    lane_8 = lax.broadcasted_iota(jnp.int32, (1, 8), 1)
    for p in range(8):
        count = jnp.sum(jnp.where(eye, counts_ref[pl.ds(p, 1), :], 0), axis=1, keepdims=True)
        rel = kept_ref[p] - 4 * flat
        code = jnp.where(rel == 0, 1, jnp.where(rel == 1, 2, jnp.where(rel == 2, 4, 8)))
        code = jnp.where((rel >= 0) & (rel < 4) & (lane < count), code, 0)
        mask = jnp.sum(code, axis=1, keepdims=True)
        h0, h1, h2 = mask & 1, (mask >> 1) & 1, (mask >> 2) & 1
        first = jnp.where(h0 == 1, 0, jnp.where(h1 == 1, 1, jnp.where(h2 == 1, 2, 3)))
        second = jnp.where(h0 + h1 == 2, 1, jnp.where((h0 + h1 == 1) & (h2 == 1), 2, 3))
        pick[0, pl.ds(8 * p, 8), :] = jnp.broadcast_to(first, (8, HD))
        pick[1, pl.ds(8 * p, 8), :] = jnp.broadcast_to(second, (8, HD))
    source = lax.broadcasted_iota(jnp.int32, (SOURCES, 256), 0)
    lane_16 = lax.broadcasted_iota(jnp.int32, (SOURCES, 256), 1)
    sx, sy = source >> 3, (source >> 2) & 1
    sz, sc = (source >> 1) & 1, source & 1
    for t in range(SLOTS):
        u, v = t // 2, t % 2
        g = 1 - 2 * c
        x0, z0, hlo, _ = pair_at(x, y, z, c, u, v)
        nx = (x + g * (2 * v - 1) + 4) % 4
        nz = (z + g * (2 * u - 1) + 4) % 4
        ny = other_y(y, odd_of(x0, z0, c))
        fx = jnp.where(sx == 0, x, nx)
        fy = jnp.where(sy == 0, y, ny)
        fz = jnp.where(sz == 0, z, nz)
        fc = jnp.where(sc == 0, c, 1 - c)
        owner = (fz * 2 + fc) * 16 + fx * 4 + fy
        p_, h_ = 2 * z0 + c, 2 * x0 + hlo
        row = kept_ref[p_, pl.ds(h_, 1), :]
        counts = jnp.where(lane_8 == h_, counts_ref[pl.ds(p_, 1), :], 0)
        live = lane_16 < jnp.sum(counts, axis=1, keepdims=True)
        here = jnp.where(live & ((row >> 2) == owner), 1, 0)
        live_keys[pl.ds(16 * t, 16), :] = jnp.broadcast_to(
            BLOCK * jnp.sum(here, axis=1, keepdims=True), (SOURCES, 2 * GROUP)
        )

    def site_of(t, cls):
        u, v = t // 2, t % 2
        dx, dy, dz, c_ = cls // 8, (cls // 4) % 2, (cls // 2) % 2, (c + cls) % 2
        g = 1 - 2 * c_
        x_ = (x - dx * g * (2 * v - 1) + 4) % 4
        z_ = (z - dz * g * (2 * u - 1) + 4) % 4
        odd = odd_of((x_ - v * g + 4) % 4, (z_ - u * g + 4) % 4, c_)
        y_ = y + dy * (other_y(y, odd) - y)
        return x_, y_, z_, c_

    def pack(t, cls, dst):
        x_, y_, z_, c_ = site_of(t, cls)
        x0, z0, hlo, _ = pair_at(x_, y_, z_, c_, t // 2, t % 2)
        part = (cls % 2) * 4 + ((cls // 2) % 2) * 2 + cls // 8
        pair = (2 * z0 + c_) * 8 + 2 * x0 + hlo
        columns = pl.ds(pl.multiple_of(hlo * HD, HD), HD)
        for slot in range(CAP):
            chosen = jnp.broadcast_to(pick[slot, pl.ds(pair, 1), :], (16, HD))
            total = [None, None]
            for block in range(slot, 4):
                weight = jnp.where(chosen == block, 1.0, 0.0).astype(jnp.bfloat16)
                weight = jnp.concatenate([weight] * (BLOCK // 16), axis=0)
                for kind in range(2):
                    rows = kv_buf[t, part, kind, pl.ds(block * BLOCK, BLOCK), columns] * weight
                    total[kind] = rows if total[kind] is None else total[kind] + rows
            for kind in range(2):
                dst[kind, pl.ds(slot * BLOCK, BLOCK), :] = total[kind]

    def pack_slot(t):
        pltpu.make_async_copy(kv_buf.at[t], kv_buf.at[t], kv_sem.at[t]).wait()

        def one(cls, carry):
            pack(t, cls, packed.at[t * 15 + cls - 1])
            return carry

        lax.fori_loop(1, SOURCES, one, 0)

    def send_slot(t):
        def one(i, carry):
            cls = (i * (5 + 2 * c)) % 16
            pltpu.make_async_remote_copy(
                src_ref=packed.at[t * 15 + cls - 1],
                dst_ref=recv.at[t, cls],
                send_sem=pack_sem,
                recv_sem=recv_sem.at[t],
                device_id=device(*site_of(t, cls)),
                device_id_type=MESH,
            ).start()
            return carry

        lax.fori_loop(1, SOURCES, one, 0)

    pack_slot(3)
    pl.semaphore_wait(barrier, 62)
    send_slot(3)
    tok_copy.start()
    wk_copy.start()
    wv_copy.start()
    for k in range(CHUNKS):
        wq_copy(k).start()
    kv_start(1)
    kv_start(0)
    pack_slot(2)
    send_slot(2)

    tok_copy.wait()
    gain_copy.wait()

    def norm(i, carry):
        rows = pl.ds(pl.multiple_of(i * 16, 16), 16)
        values = tok[rows, :].astype(jnp.float32)
        mean_square = jnp.mean(values * values, axis=-1, keepdims=True)
        normed[rows, :] = (values * lax.rsqrt(mean_square + 1e-05) * gain_ref[...]).astype(
            jnp.bfloat16
        )
        return carry

    lax.fori_loop(0, STEPS // 16, norm, 0)
    wk_copy.wait()
    wv_copy.wait()
    n_acc[...] = jnp.zeros_like(n_acc)
    q_acc[...] = jnp.zeros_like(q_acc)

    def project(k, carry):
        columns = pl.ds(pl.multiple_of(k * CHUNK, CHUNK), CHUNK)
        wq_copy(k).wait()
        rows = normed[:, columns]
        q_acc[...] += jnp.dot(rows, wq[columns, :], preferred_element_type=jnp.float32)
        n_acc[...] += lax.dot_general(rows, wkv[:, columns], NT, preferred_element_type=jnp.float32)
        return carry

    lax.fori_loop(0, CHUNKS, project, 0)

    mine = n_acc[...].astype(jnp.bfloat16)
    piece[...] = mine
    piece_copy = pltpu.make_async_remote_copy(
        src_ref=piece,
        dst_ref=other,
        send_sem=piece_sem.at[0],
        recv_sem=piece_sem.at[1],
        device_id=device(x, y + 1 - 2 * (y % 2), z, c),
        device_id_type=MESH,
    )
    piece_copy.start()
    for g in range(4):
        q_send[pl.ds(g * STEPS, STEPS), :] = q_acc[:, g * HD : (g + 1) * HD].astype(jnp.bfloat16)
    half = y % 2
    toward = 1 - 2 * c
    shift = odd_of(x, z, c) * (1 + 2 * c)

    def site_y(i):
        return (2 * (y // 2) + (i // 2) % 2 - shift + 4) % 4

    def q_copy(i):
        bx, bz = i // 4, i % 2
        return pltpu.make_async_remote_copy(
            src_ref=q_send,
            dst_ref=q_buf.at[2 * bz + bx, half],
            send_sem=q_send_sem.at[i],
            recv_sem=q_recv_sem.at[2 * bz + bx, half],
            device_id=device(
                (x + bx * toward + 4) % 4, site_y(i), (z + bz * toward + 4) % 4, c
            ),
            device_id_type=MESH,
        )

    def is_self(i):
        return (i // 4 == 0) & (i % 2 == 0) & (site_y(i) == y)

    def q_start(i, carry):
        @pl.when(jnp.logical_not(is_self(i)))
        def _():
            q_copy(i).start()

        @pl.when(is_self(i))
        def _():
            q_buf[0, half] = q_send[...]

        return carry

    lax.fori_loop(0, SITES, q_start, 0)

    for t in (1, 0):
        pack_slot(t)
        send_slot(t)

    piece_copy.wait()
    mine = piece[...].astype(jnp.float32)
    theirs = other[...].astype(jnp.float32)
    low = jnp.where(half == 0, mine, theirs)
    high = jnp.where(half == 0, theirs, mine)
    first_half = lax.broadcasted_iota(jnp.int32, (STEPS, HD), 1) < 64
    new_keys = jnp.where(first_half, low, pltpu.roll(high, 64, 1)).astype(jnp.bfloat16)
    new_values = jnp.where(first_half, pltpu.roll(low, 64, 1), high).astype(jnp.bfloat16)
    ent_ref[pl.ds(0, STEPS), :] = new_keys
    ent_ref[pl.ds(STEPS, STEPS), :] = new_values
    scores = lax.dot_general(new_keys, q_send[...], NT, preferred_element_type=jnp.float32)
    key_step = lax.broadcasted_iota(jnp.int32, (STEPS, GROUP), 0)
    row_step = lax.broadcasted_iota(jnp.int32, (STEPS, GROUP), 1) % STEPS
    scores = jnp.where(key_step <= row_step, scores, LOWEST)
    top = jnp.max(scores, axis=0, keepdims=True)
    weights = jnp.exp2((scores - top) * EXP_SCALE)
    own_l[...] = jnp.broadcast_to(
        top * EXP_SCALE + jnp.log2(jnp.sum(weights, axis=0, keepdims=True)), (8, GROUP)
    )
    own_o[...] = lax.dot_general(
        new_values, weights.astype(jnp.bfloat16), TN, preferred_element_type=jnp.float32
    ) / jnp.sum(weights, axis=0, keepdims=True)

    key_row = lax.broadcasted_iota(jnp.int32, (KEYS, 2 * GROUP), 0)

    def home_of(t):
        u, v = t // 2, t % 2
        x0, z0, hlo, by = pair_at(x, y, z, c, u, v)
        near = (t == 0) & (hlo == y // 2)
        return x0, z0, hlo, near, v * 4 + by * 2 + u

    def out_copies(t, m):
        x0, z0, hlo, _, site = home_of(t)
        home = device(x0, 2 * hlo + m, z0, c)
        return (
            pltpu.make_async_remote_copy(
                src_ref=o_send.at[t, m],
                dst_ref=o_buf.at[site],
                send_sem=o_send_sem.at[t, m],
                recv_sem=o_recv_sem.at[site],
                device_id=home,
                device_id_type=MESH,
            ),
            pltpu.make_async_remote_copy(
                src_ref=l_send.at[t, m, pl.ds(0, 1)],
                dst_ref=l_buf.at[site, pl.ds(0, 1)],
                send_sem=l_send_sem.at[t, m],
                recv_sem=l_recv_sem.at[site],
                device_id=home,
                device_id_type=MESH,
            ),
        )

    def attend(step, carry):
        t = SLOTS - 1 - step
        x0, z0, hlo, near, site = home_of(t)
        for m in range(2):

            @pl.when(jnp.logical_not(near & (y % 2 == m)))
            def _(m=m):
                pltpu.make_async_copy(
                    q_buf.at[t, m], q_buf.at[t, m], q_recv_sem.at[t, m]
                ).wait()

        arrived = recv.at[t, pl.ds(1, SOURCES - 1)]
        pltpu.make_async_copy(arrived, arrived, recv_sem.at[t]).wait()
        pack(t, 0, recv.at[t, 0])
        q = q_buf[t].reshape(2 * GROUP, HD)

        keys = recv[t, :, 0].reshape(SOURCES * KEYS, HD)
        values = recv[t, :, 1].reshape(SOURCES * KEYS, HD)
        s = lax.dot_general(keys, q, NT, preferred_element_type=jnp.float32)
        s = jnp.concatenate(
            [
                jnp.where(
                    key_row < live_keys[pl.ds(16 * t + i, 1), :],
                    s[i * KEYS : (i + 1) * KEYS],
                    LOWEST,
                )
                for i in range(SOURCES)
            ],
            axis=0,
        )
        top = jnp.max(s, axis=0, keepdims=True)
        w = jnp.exp2((s - top) * EXP_SCALE)
        total = jnp.sum(w, axis=0, keepdims=True)
        o = lax.dot_general(
            values, w.astype(jnp.bfloat16), TN, preferred_element_type=jnp.float32
        )
        o = (o / total).astype(jnp.bfloat16)
        lse = jnp.broadcast_to(top * EXP_SCALE + jnp.log2(total), (8, 2 * GROUP))
        for m in range(2):
            o_send[t, m] = o[:, m * GROUP : (m + 1) * GROUP]
            l_send[t, m] = lse[:, m * GROUP : (m + 1) * GROUP]
            leaves = jnp.logical_not(near & (y % 2 == m))

            @pl.when(leaves)
            def _(m=m):
                for copy in out_copies(t, m):
                    copy.start()

            @pl.when(jnp.logical_not(leaves))
            def _(m=m):
                o_buf[site] = o_send[t, m]
                l_buf[site] = l_send[t, m]

        return carry

    lax.fori_loop(0, SLOTS, attend, 0)

    def await_site(i):
        @pl.when(jnp.logical_not(is_self(i)))
        def _():
            pltpu.make_async_copy(o_buf.at[i], o_buf.at[i], o_recv_sem.at[i]).wait()
            row = l_buf.at[i, pl.ds(0, 1)]
            pltpu.make_async_copy(row, row, l_recv_sem.at[i]).wait()

    top, total, result = own_l[pl.ds(0, 1), :], jnp.ones((1, GROUP), jnp.float32), own_o[...]
    for sites in ((1, 3, 4, 5, 6, 7), (0, 2)):
        for i in sites:
            await_site(i)
        old_top = top
        for i in sites:
            top = jnp.maximum(top, l_buf[i, pl.ds(0, 1), :])
        share = jnp.exp2(old_top - top)
        total, result = total * share, result * share
        for i in sites:
            share = jnp.exp2(l_buf[i, pl.ds(0, 1), :] - top)
            total = total + share
            result = result + o_buf[i].astype(jnp.float32) * share
    result = (result / total).T
    for g in range(4):
        att_ref[:, g * HD : (g + 1) * HD] = result[g * STEPS : (g + 1) * STEPS, :].astype(
            jnp.bfloat16
        )

    pltpu.make_async_copy(packed, packed, pack_sem).wait()

    def await_q(i, carry):
        @pl.when(jnp.logical_not(is_self(i)))
        def _():
            q_copy(i).wait_send()

        return carry

    lax.fori_loop(0, SITES, await_q, 0)

    def await_out(t, carry):
        _, _, _, near, _ = home_of(t)
        for m in range(2):

            @pl.when(jnp.logical_not(near & (y % 2 == m)))
            def _(m=m):
                for copy in out_copies(t, m):
                    copy.wait_send()

        return carry

    lax.fori_loop(0, SLOTS, await_out, 0)


def place(att_ref, ent_ref, att_out, ent_out):
    att_out[...] = att_ref[...]
    for row in range(2 * STEPS):
        ent_out[0, :, row * HD : (row + 1) * HD] = ent_ref[row : row + 1, :]


def per_device(
    new_tokens,
    norm_gain,
    query_weight,
    key_weight,
    value_weight,
    kv_cache,
    kept_blocks,
    kept_counts,
):
    vmem = pl.BlockSpec(memory_space=pltpu.VMEM)
    hbm = pl.BlockSpec(memory_space=pl.ANY)
    bf16, f32 = jnp.bfloat16, jnp.float32
    dma = pltpu.SemaphoreType.DMA
    attended, entries = pl.pallas_call(
        kernel,
        out_shape=(
            jax.ShapeDtypeStruct((STEPS, 4 * HD), bf16),
            jax.ShapeDtypeStruct((2 * STEPS, HD), bf16),
        ),
        in_specs=[hbm] * 8,
        out_specs=(vmem, vmem),
        scratch_shapes=[
            pltpu.VMEM((1, WIDTH), f32),
            pltpu.VMEM((8, 8, 256), jnp.int32),
            pltpu.VMEM((8, 8), jnp.int32),
            pltpu.VMEM((SLOTS, 8, 2, TOKD, 2 * HD), bf16),
            pltpu.VMEM((SLOTS * (SOURCES - 1), 2, KEYS, HD), bf16),
            pltpu.VMEM((SLOTS, SOURCES, 2, KEYS, HD), bf16),
            pltpu.VMEM((STEPS, WIDTH), bf16),
            pltpu.VMEM((STEPS, WIDTH), bf16),
            pltpu.VMEM((WIDTH, 4 * HD), bf16),
            pltpu.VMEM((HD, WIDTH), bf16),
            pltpu.VMEM((STEPS, 4 * HD), f32),
            pltpu.VMEM((STEPS, HD), f32),
            pltpu.VMEM((GROUP, HD), bf16),
            pltpu.VMEM((SLOTS, 2, GROUP, HD), bf16),
            pltpu.VMEM((CAP, 64, HD), jnp.int32),
            pltpu.VMEM((SLOTS * SOURCES, 2 * GROUP), jnp.int32),
            pltpu.VMEM((SLOTS, 2, HD, GROUP), bf16),
            pltpu.VMEM((SLOTS, 2, 8, GROUP), f32),
            pltpu.VMEM((SITES, HD, GROUP), bf16),
            pltpu.VMEM((SITES, 8, GROUP), f32),
            pltpu.VMEM((HD, GROUP), f32),
            pltpu.VMEM((8, GROUP), f32),
            pltpu.VMEM((STEPS, HD), bf16),
            pltpu.VMEM((STEPS, HD), bf16),
            dma((SLOTS,)),
            dma((CHUNKS + 2,)),
            dma,
            dma((3,)),
            dma,
            dma((SLOTS,)),
            dma((SITES,)),
            dma((SLOTS, 2)),
            dma((SLOTS, 2)),
            dma((SITES,)),
            dma((SLOTS, 2)),
            dma((SITES,)),
            dma((2,)),
        ],
        compiler_params=pltpu.CompilerParams(
            collective_id=0, has_side_effects=True, vmem_limit_bytes=56 * 1024 * 1024
        ),
    )(
        new_tokens.reshape(STEPS, WIDTH),
        norm_gain.reshape(1, WIDTH),
        query_weight,
        key_weight.T,
        value_weight.T,
        kv_cache,
        kept_blocks,
        kept_counts,
    )
    attended, entries = pl.pallas_call(
        place,
        out_shape=(
            jax.ShapeDtypeStruct((STEPS, 4 * HD), bf16),
            jax.ShapeDtypeStruct((1, 1, 2 * STEPS * HD), bf16),
        ),
        in_specs=[vmem, vmem],
        out_specs=(vmem, vmem),
    )(attended, entries)
    return attended.reshape(STEPS, 1, 4 * HD), entries


def solution(mesh):
    in_specs = (
        P(None, "seq", None),
        P(),
        P(None, "tp"),
        P(None, "tp"),
        P(None, "tp"),
        P(None, None, ("seq", "tp"), None),
        P(),
        P(),
    )
    out_specs = (P(None, "seq", "tp"), P("seq", "tp", None))
    return jax.shard_map(
        per_device, mesh=mesh, in_specs=in_specs, out_specs=out_specs, check_vma=False
    )
```
